128 devices in a mesh: fsdp: 16 (over x, z_hi, core), rep: 8 (over y, z_lo).
Axes of the slice: x: 4, y: 4, z: 4 (z_hi: 2, z_lo: 2; z = z_hi * 2 + z_lo), core: 2. Of those that a mesh axis runs over, the one named last changes fastest.
Arguments:
- tokens: bfloat16 [65536, 1536], P(('fsdp', 'rep')), may hold values from -6 to 6
- weight: float32 [6144, 1536], P('fsdp'), may hold values from -0.15625 to 0.15625
- cotangent: bfloat16 [65536, 6144], P(('fsdp', 'rep')), may hold values from -24 to 24
Outputs:
- activated: bfloat16 [65536, 6144], P(('fsdp', 'rep'))
- input_grad: float32 [65536, 1536], P(('fsdp', 'rep'))
- weight_grad: float32 [6144, 1536], P('fsdp')
The draws below stay inside these ranges and needn't reach their ends.
All inputs are finite; a program needn't handle non-finite values.
Results may differ from the reference program's by a relative error of at most 0.022.
Values may be sent and summed in bfloat16 or wider, within the bound.
No kernel may reach another device: no remote copies, remote signals or barrier semaphores. Data moves between devices by JAX's collectives and lax.ppermute only.
A program may use at most 192 MiB of HBM per device.

```python
import math
import jax
import jax.numpy as jnp
from jax import lax

D = 1536
F = 6144
TOK_DEV = 512
TOKENS = 65536


def raised(array, key, source, target, shards_of, factor):
    owner, partner = [(jnp.arange(array.shape[axis_at]) // (array.shape[axis_at] // shards_of)).reshape([-1 if axis == axis_at else 1 for axis in range(array.ndim)]) for axis_at in (source, target)]
    chosen = jax.random.permutation(key, shards_of)[partner]
    strong = (owner == chosen) | (owner == (partner + shards_of // 2) % shards_of)
    return jnp.where(strong, factor * array, array)


def steps_of(rng, shape, shards, least, top_value):
    def one(position, parts):
        heights = jax.random.uniform(jax.random.fold_in(jax.random.fold_in(rng, 6), position), (parts,), jnp.float32, least / len(shards), top_value / len(shards))
        return jnp.repeat(jnp.exp(heights), shape[position] // parts).reshape((-1,) + (1,) * (len(shape) - position - 1))

    level = one(*shards[0])
    for cut in shards[1:]:
        level = level * one(*cut)
    return level


def gaussian(rng, extent, scale, limit, pieces=(), kind=jnp.bfloat16):
    entries = scale * jax.random.normal(rng, extent, jnp.float32)
    if pieces:
        entries = entries * steps_of(rng, extent, pieces, -0.22, 0.18)
    return jnp.clip(entries, -limit, limit).astype(kind)


def gaussian_with(rng, dims, scale, most, shards, heavy, kind=jnp.bfloat16):
    drawn = scale * jax.random.normal(rng, dims, jnp.float32)
    if shards:
        drawn = drawn * steps_of(rng, dims, shards, -0.22, 0.18)
    return jnp.clip(raised(drawn, jax.random.fold_in(rng, 3), *heavy), -most, most).astype(kind)


def setup_inputs(seed: int = 0) -> dict:
    keys = jax.random.split(jax.random.key(seed), 4)
    tokens = gaussian(keys[0], (TOKENS, D), 1.0, 6.0, ((0, 128),))
    weight = gaussian(keys[1], (F, D), D ** -0.5, 0.15625, ((0, 16),), jnp.float32)
    cotangent = gaussian_with(keys[2], (TOKENS, F), 1.0, 24.0, ((0, 128),), (0, 1, 128, 5.5))
    return {"tokens": tokens, "weight": weight, "cotangent": cotangent}


def gelu_tanh(value):
    return jax.nn.gelu(value, approximate=True)

def block_pass(weight_b, token_block, cot_block):
    pre = lax.dot_general(token_block, weight_b, (((1,), (1,)), ((), ())), preferred_element_type=jnp.float32)
    activated, pullback = jax.vjp(gelu_tanh, pre)
    slope_grad = pullback(cot_block.astype(jnp.float32))[0].astype(jnp.bfloat16)
    input_grad = jnp.dot(slope_grad, weight_b, preferred_element_type=jnp.float32)
    return (activated.astype(jnp.bfloat16), slope_grad, input_grad)

def reference(tokens, weight, cotangent):
    weight_b = weight.astype(jnp.bfloat16)
    scale = jnp.float32(1.0 / math.sqrt(TOKENS))
    blocks = TOKENS // TOK_DEV
    token_blocks = tokens.reshape(blocks, TOK_DEV, D)
    cot_blocks = cotangent.reshape(blocks, TOK_DEV, F)

    def step(total, pair):
        token_block, cot_block = pair
        activated, slope_grad, input_grad = block_pass(weight_b, token_block, cot_block)
        term = lax.dot_general(slope_grad, token_block, (((0,), (0,)), ((), ())), preferred_element_type=jnp.float32) * scale
        rounded = lax.optimization_barrier(term.astype(jnp.bfloat16))
        return (total + rounded.astype(jnp.float32), (activated, input_grad))
    start = jnp.zeros((F, D), jnp.float32)
    weight_grad, outputs = lax.scan(step, start, (token_blocks, cot_blocks))
    activated = outputs[0].reshape(TOKENS, F)
    input_grad = outputs[1].reshape(TOKENS, D)
    return (activated, input_grad, weight_grad)
```

```python
import functools
import math

import jax
import jax.numpy as jnp
from jax import lax
from jax.experimental import pallas as pl
from jax.experimental.pallas import tpu as pltpu
from jax.sharding import PartitionSpec as P

BF = jnp.bfloat16
F32 = jnp.float32
NX, NY = 4, 4
TILE = 256
ROLES = ("own", "a", "b", "own_z", "ab", "a_z", "b_z", "ab_z")


def coords(f, r):
    return f // 4, r // 2, (f // 2) % 2, r % 2, f % 2


def permute(value, target):
    pairs = []
    for i in range(128):
        x, y, zh, zl, c = target(*coords(i // 8, i % 8))
        pairs.append((i, (x * 4 + zh * 2 + c) * 8 + y * 2 + zl))
    return lax.ppermute(value, ("fsdp", "rep"), pairs)


def first(i, c):
    return i ^ 1 if c == 0 else 3 - i


def second(i, c):
    return first(i, 1 - c)


def x_first(v):
    return permute(v, lambda x, y, zh, zl, c: (first(x, c), y, zh, zl, c))


def x_second(v):
    return permute(v, lambda x, y, zh, zl, c: (second(x, c), y, zh, zl, c))


def y_first(v):
    return permute(v, lambda x, y, zh, zl, c: (x, first(y, c), zh, zl, c))


def y_second(v):
    return permute(v, lambda x, y, zh, zl, c: (x, second(y, c), zh, zl, c))


def z_outer(v):
    return permute(v, lambda x, y, zh, zl, c: (x, y, 1 - zh, 1 - zl, c))


def z_inner(v):
    return permute(v, lambda x, y, zh, zl, c: (x, y, zh, 1 - zl, c))


def other_core(v):
    return permute(v, lambda x, y, zh, zl, c: (x, y, zh, zl, 1 - c))


def add(a, b):
    return (a.astype(F32) + b.astype(F32)).astype(BF)


def rows_of(v, part, parts):
    n = v.shape[0] // parts
    return lax.dynamic_slice_in_dim(v, part * n, n, 0)


def block_kernel(halves, scale, n_alias, at, tok_o, tok_p, *refs):
    n_w = 2 if halves else 1
    w_in = refs[:n_w]
    cot_o, cot_p = refs[n_w : n_w + 2]
    act_o, act_p, slope_o, w_o, send_o, keep_o, acc = refs[n_w + 2 + n_alias :]
    i = pl.program_id(0)
    n_own = pl.num_programs(0) // 2

    @pl.when(i == 0)
    def _():
        if halves:
            n = w_in[0].shape[0]
            here = pl.multiple_of(at[3] * n, n)
            there = pl.multiple_of((1 - at[3]) * n, n)
            w_o[pl.ds(here, n), :] = w_in[0][...]
            w_o[pl.ds(there, n), :] = w_in[1][...]
        else:
            w_o[...] = w_in[0][...]

    def tile(tok, cot, act):
        pre = lax.dot_general(tok[...], w_o[...], (((1,), (1,)), ((), ())), preferred_element_type=F32)
        k = math.sqrt(2.0 / math.pi)
        square = pre * pre
        t = jnp.tanh(k * (pre + 0.044715 * (pre * square)))
        half = 0.5 * (1.0 + t)
        act[...] = (pre * half).astype(BF)
        slope = half + 0.5 * pre * (1.0 - t * t) * (k * (1.0 + 3 * 0.044715 * square))
        slope = (cot[...].astype(F32) * slope).astype(BF)
        slope_o[...] = slope
        term = lax.dot_general(slope, tok[...], (((0,), (0,)), ((), ())), preferred_element_type=F32)

        @pl.when(i == 0)
        def _():
            acc[...] = term

        @pl.when(i > 0)
        def _():
            acc[...] += term

    @pl.when(i < n_own)
    def _():
        tile(tok_o, cot_o, act_o)

    @pl.when(i >= n_own)
    def _():
        tile(tok_p, cot_p, act_p)

    @pl.when(i == pl.num_programs(0) - 1)
    def _():
        n = keep_o.shape[0]
        keep = pl.multiple_of(at[2] * n, n)
        send = pl.multiple_of((1 - at[2]) * n, n)
        keep_o[...] = (acc[pl.ds(keep, n), :] * scale).astype(BF)
        send_o[...] = (acc[pl.ds(send, n), :] * scale).astype(BF)


def block(role, at, tok_o, tok_p, ws, cot_o, cot_p, bufs, scale):
    m, d = tok_o.shape
    rows = 384
    n_all = cot_p.shape[1]
    n_own = m // TILE
    low = lambda i: jnp.minimum(i, n_own - 1)
    high = lambda i: jnp.maximum(i - n_own, 0)
    w_specs = [pl.BlockSpec(w.shape, lambda i, at: (0, 0)) for w in ws]
    alias_args = [] if bufs is None else list(bufs)
    n_alias = len(alias_args)
    before = 1 + 2 + len(ws) + 2
    out = pl.pallas_call(
        functools.partial(block_kernel, len(ws) == 2, scale, n_alias),
        grid_spec=pltpu.PrefetchScalarGridSpec(
            num_scalar_prefetch=1,
            grid=(2 * n_own,),
            in_specs=[
                pl.BlockSpec((TILE, d), lambda i, at: (low(i), 0)),
                pl.BlockSpec((TILE, d), lambda i, at: (high(i), 0)),
                *w_specs,
                pl.BlockSpec((TILE, rows), lambda i, at: (low(i), at[0])),
                pl.BlockSpec((TILE, rows), lambda i, at: (high(i), at[1])),
                *([pl.BlockSpec(memory_space=pl.ANY)] * n_alias),
            ],
            out_specs=[
                pl.BlockSpec((TILE, rows), lambda i, at: (low(i), at[0])),
                pl.BlockSpec((TILE, rows), lambda i, at: (high(i), at[1])),
                pl.BlockSpec((TILE, rows), lambda i, at: (i, role)),
                pl.BlockSpec((rows, d), lambda i, at: (role, 0)),
                pl.BlockSpec((rows // 2, d), lambda i, at: (0, 0)),
                pl.BlockSpec((rows // 2, d), lambda i, at: (0, 0)),
            ],
            scratch_shapes=[pltpu.VMEM((rows, d), F32)],
        ),
        out_shape=[
            jax.ShapeDtypeStruct((m, 2 * n_all), BF),
            jax.ShapeDtypeStruct((m, n_all), BF),
            jax.ShapeDtypeStruct((2 * m, n_all), BF),
            jax.ShapeDtypeStruct((n_all, d), BF),
            jax.ShapeDtypeStruct((rows // 2, d), BF),
            jax.ShapeDtypeStruct((rows // 2, d), BF),
        ],
        input_output_aliases={before + j: j for j in range(n_alias)},
        compiler_params=pltpu.CompilerParams(
            dimension_semantics=("arbitrary",), vmem_limit_bytes=32 * 1024 * 1024
        ),
        cost_estimate=pl.CostEstimate(
            flops=2 * 2 * 2 * m * rows * d, bytes_accessed=10 * rows * d * 2, transcendentals=2 * m * rows
        ),
        name=f"block_{role}",
    )(at, tok_o, tok_p, *ws, cot_o, cot_p, *alias_args)
    return out[:4], out[4], out[5]


def copy_kernel(at, src, *refs):
    refs[-1][...] = src[...]


def pack(cot, c, rows):
    m, n = cot.shape
    return pl.pallas_call(
        copy_kernel,
        grid_spec=pltpu.PrefetchScalarGridSpec(
            num_scalar_prefetch=1,
            grid=(n // rows // 2,),
            in_specs=[pl.BlockSpec((m, rows), lambda i, at: (0, 2 * i + 1 - at[0]))],
            out_specs=pl.BlockSpec((m, rows), lambda i, at: (0, i)),
        ),
        out_shape=jax.ShapeDtypeStruct((m, n // 2), BF),
        name="pack",
    )(c[None], cot)


def unpack(act, received, c, rows):
    m, n = act.shape
    return pl.pallas_call(
        copy_kernel,
        grid_spec=pltpu.PrefetchScalarGridSpec(
            num_scalar_prefetch=1,
            grid=(n // rows // 2,),
            in_specs=[pl.BlockSpec((m, rows), lambda i, at: (0, i)), pl.BlockSpec(memory_space=pl.ANY)],
            out_specs=pl.BlockSpec((m, rows), lambda i, at: (0, 2 * i + 1 - at[0])),
        ),
        out_shape=jax.ShapeDtypeStruct((m, n), BF),
        input_output_aliases={2: 0},
        name="unpack",
    )(c[None], received, act)


def local(tokens, weight, cotangent):
    rows = weight.shape[0]
    f, r = lax.axis_index("fsdp"), lax.axis_index("rep")
    x, y, zh, zl, c = coords(f, r)
    total_tokens = tokens.shape[0] * lax.axis_size("fsdp") * lax.axis_size("rep")
    scale = 1.0 / math.sqrt(total_tokens)

    own = weight.astype(BF)
    tok_p = other_core(tokens)
    w = {"own": [own]}
    w["a"] = [x_first(own)]
    w["b"] = [x_second(own)]
    cot_p = other_core(pack(cotangent, c, rows))

    def z_gather(v):
        near = z_outer(rows_of(v, 1 - zl, 2))
        return [near, z_inner(near)]

    w["own_z"] = z_gather(own)
    w["ab"] = [x_second(w["a"][0])]
    w["a_z"] = z_gather(w["a"][0])
    w["b_z"] = z_gather(w["b"][0])
    w["ab_z"] = [x_second(v) for v in w["a_z"]]

    xa = jnp.where(c == 0, x ^ 1, 3 - x)
    xb = jnp.where(c == 0, 3 - x, x ^ 1)
    at_x = {"own": x, "a": xa, "b": xb, "ab": (x + 2) % 4}
    y0, y1 = y % 2, y // 2
    y_half = jnp.where(c == 0, y0 ^ y1, y1)
    y_part = jnp.where(c == 0, y1, y0)

    bufs = None
    sums = {}
    for role, name in enumerate(ROLES):
        there = 2 * at_x[name.removesuffix("_z")] + (1 - zh if name.endswith("_z") else zh)
        at = jnp.stack([2 * there + c, there, y_half, zl]).astype(jnp.int32)
        bufs, send, keep = block(role, at, tokens, tok_p, w[name], cotangent, cot_p, bufs, scale)
        half = add(keep, y_first(send))
        sums[name] = add(rows_of(half, y_part, 2), y_second(rows_of(half, 1 - y_part, 2)))
    act, act_p, slope, w_all = bufs

    def x_sum(end):
        got = x_first(jnp.concatenate([sums["a" + end], sums["ab" + end]]))
        n = got.shape[0] // 2
        rest = add(sums["b" + end], got[n:])
        return add(add(sums["own" + end], got[:n]), x_second(rest))

    same, other = x_sum(""), x_sum("_z")
    k = zh ^ zl
    got = z_inner(jnp.concatenate([rows_of(same, 1 - k, 2), rows_of(other, 1 - k, 2)]))
    n = got.shape[0] // 2
    same, other = add(rows_of(same, k, 2), got[:n]), add(rows_of(other, k, 2), got[n:])
    piece = add(same, z_outer(other))

    pair = z_inner(piece)
    quarter = jnp.where(k == 0, jnp.concatenate([piece, pair]), jnp.concatenate([pair, piece]))
    q2 = y_second(quarter)
    half = jnp.where(y_part == 0, jnp.concatenate([quarter, q2]), jnp.concatenate([q2, quarter]))
    h2 = y_first(half)
    weight_grad = jnp.where(y_half == 0, jnp.concatenate([half, h2]), jnp.concatenate([h2, half])).astype(F32)

    activated = unpack(act, other_core(act_p), c, rows)
    grad = jnp.dot(slope, w_all, preferred_element_type=F32)
    m = tokens.shape[0]
    input_grad = grad[:m] + other_core(grad[m:])
    return activated, input_grad, weight_grad


def solution(mesh):
    in_specs = (P(("fsdp", "rep"), None), P("fsdp", None), P(("fsdp", "rep"), None))
    out_specs = (P(("fsdp", "rep"), None), P(("fsdp", "rep"), None), P("fsdp", None))
    return jax.shard_map(local, mesh=mesh, in_specs=in_specs, out_specs=out_specs, check_vma=False)
```

```python
import functools
import math

import jax
import jax.numpy as jnp
from jax import lax
from jax.experimental import pallas as pl
from jax.experimental.pallas import tpu as pltpu
from jax.sharding import PartitionSpec as P

BF = jnp.bfloat16
F32 = jnp.float32
NX, NY = 4, 4
TILE = 256
ROLES = ("own", "a", "b", "own_z", "ab", "a_z", "b_z", "ab_z")


def coords(f, r):
    return f // 4, r // 2, (f // 2) % 2, r % 2, f % 2


def permute(value, target):
    pairs = []
    for i in range(128):
        x, y, zh, zl, c = target(*coords(i // 8, i % 8))
        pairs.append((i, (x * 4 + zh * 2 + c) * 8 + y * 2 + zl))
    return lax.ppermute(value, ("fsdp", "rep"), pairs)


def first(i, c):
    return i ^ 1 if c == 0 else 3 - i


def second(i, c):
    return first(i, 1 - c)


def x_first(v):
    return permute(v, lambda x, y, zh, zl, c: (first(x, c), y, zh, zl, c))


def x_second(v):
    return permute(v, lambda x, y, zh, zl, c: (second(x, c), y, zh, zl, c))


def y_first(v):
    return permute(v, lambda x, y, zh, zl, c: (x, first(y, c), zh, zl, c))


def y_second(v):
    return permute(v, lambda x, y, zh, zl, c: (x, second(y, c), zh, zl, c))


def z_outer(v):
    return permute(v, lambda x, y, zh, zl, c: (x, y, 1 - zh, 1 - zl, c))


def z_inner(v):
    return permute(v, lambda x, y, zh, zl, c: (x, y, zh, 1 - zl, c))


def z_across(v):
    return permute(v, lambda x, y, zh, zl, c: (x, y, 1 - zh, zl, c))


def other_core(v):
    return permute(v, lambda x, y, zh, zl, c: (x, y, zh, zl, 1 - c))


def add(a, b):
    return (a.astype(F32) + b.astype(F32)).astype(BF)


def gelu_and_slope(pre, cot):
    k = math.sqrt(2.0 / math.pi)
    square = pre * pre
    t = jnp.tanh(pre * (k + (k * 0.044715) * square))
    half = 0.5 + 0.5 * t
    act = pre * half
    slope = half + (act - act * t) * (k + (3 * k * 0.044715) * square)
    return act.astype(BF), (cot.astype(F32) * slope).astype(BF)


def block_kernel(role, scale, n_w, n_alias, sums, at, tok_o, tok_p, *refs):
    w_in, (cot_o, cot_p), earlier = refs[:n_w], refs[n_w : n_w + 2], refs[n_w + 2 : n_w + 2 + 2 * sums]
    act_o, act_p, slope_o, w, send_o, keep_o, *quarter_o = refs[n_w + 2 + 2 * sums + n_alias :]
    n = w.shape[0] // 2
    far_in, near_in = w_in if n_w == 2 else (w_in[0].at[:n], w_in[0].at[n:])
    w[pl.ds(pl.multiple_of(at[role, 3] * n, n), n), :] = near_in[...]
    w[pl.ds(pl.multiple_of((1 - at[role, 3]) * n, n), n), :] = far_in[...]
    m = tok_o.shape[0]
    for j, (tok, cot, act) in enumerate(((tok_o, cot_o, act_o), (tok_p, cot_p, act_p))):
        for s in range(0, m, TILE):
            r = slice(s, s + TILE)
            pre = lax.dot_general(tok[r], w[...], (((1,), (1,)), ((), ())), preferred_element_type=F32)
            act[r], slope_o[j * m + s : j * m + s + TILE] = gelu_and_slope(pre, cot[r])
    if sums:
        keep, got = earlier
        n = quarter_o[0].shape[1]
        cols = pl.ds(pl.multiple_of((1 - at[role, 4]) * n, n), n)
        quarter_o[0][...] = (keep[:, cols].astype(F32) + got[:, cols].astype(F32)).astype(BF)
    n = keep_o.shape[1]
    for out, half in ((send_o, 1 - at[role, 2]), (keep_o, at[role, 2])):
        cols = pl.ds(pl.multiple_of(half * n, n), n)
        tok = jnp.concatenate([tok_o[:, cols], tok_p[:, cols]], axis=0)
        term = lax.dot_general(slope_o[...], tok, (((0,), (0,)), ((), ())), preferred_element_type=F32)
        out[...] = (term * scale).astype(BF)


def block(role, at, tok_o, tok_p, w, cot_o, cot_p, earlier, bufs, scale):
    m, d = tok_o.shape
    rows = sum(v.shape[0] for v in w)
    n_all = cot_o.shape[1]
    sums = bool(earlier)
    whole = lambda *shape: pl.BlockSpec(shape, lambda i, at: (0, 0))
    before = 1 + 4 + len(w) + len(earlier)
    half, quarter = (rows, d // 2), (rows, d // 4)
    small = [half, half] + [quarter] * sums
    out = pl.pallas_call(
        functools.partial(block_kernel, role, scale, len(w), len(bufs), sums),
        grid_spec=pltpu.PrefetchScalarGridSpec(
            num_scalar_prefetch=1,
            grid=(1,),
            in_specs=[
                whole(m, d),
                whole(m, d),
                *[whole(*v.shape) for v in w],
                pl.BlockSpec((m, rows), lambda i, at: (0, at[role, 0])),
                pl.BlockSpec((m, rows), lambda i, at: (0, at[role, 0])),
                *([whole(*half)] * len(earlier)),
                *([pl.BlockSpec(memory_space=pl.ANY)] * len(bufs)),
            ],
            out_specs=[
                pl.BlockSpec((m, rows), lambda i, at: (0, at[role, 0])),
                pl.BlockSpec((m, rows), lambda i, at: (0, at[role, 1])),
                pl.BlockSpec((2 * m, rows), lambda i, at: (0, role)),
                pl.BlockSpec((rows, d), lambda i, at: (role, 0)),
                *[whole(*s) for s in small],
            ],
        ),
        out_shape=[
            jax.ShapeDtypeStruct((m, n_all), BF),
            jax.ShapeDtypeStruct((m, n_all // 2), BF),
            jax.ShapeDtypeStruct((2 * m, n_all // 2), BF),
            jax.ShapeDtypeStruct((n_all // 2, d), BF),
            *[jax.ShapeDtypeStruct(s, BF) for s in small],
        ],
        input_output_aliases={before + j: j for j in range(len(bufs))},
        compiler_params=pltpu.CompilerParams(vmem_limit_bytes=56 * 1024 * 1024),
        cost_estimate=pl.CostEstimate(
            flops=4 * 2 * m * rows * d, bytes_accessed=16 * rows * d, transcendentals=2 * m * rows
        ),
        name=f"block_{role}",
    )(at, tok_o, tok_p, *w, cot_o, cot_p, *earlier, *bufs)
    return out[:4], *out[4:]


def round_kernel(at, far, near, far_o, near_o, both_o):
    n = far.shape[0]
    far_o[...] = both_o[:n] = far[...].astype(BF)
    near_o[...] = both_o[n:] = near[...].astype(BF)


def rounded(zl, weight):
    rows, d = weight.shape
    whole = lambda *shape: pl.BlockSpec(shape, lambda i, at: (0, 0))
    shapes = [(rows // 2, d), (rows // 2, d), (rows, d)]
    return pl.pallas_call(
        round_kernel,
        grid_spec=pltpu.PrefetchScalarGridSpec(
            num_scalar_prefetch=1,
            grid=(1,),
            in_specs=[
                pl.BlockSpec((rows // 2, d), lambda i, at: (1 - at[0], 0)),
                pl.BlockSpec((rows // 2, d), lambda i, at: (at[0], 0)),
            ],
            out_specs=[whole(*s) for s in shapes],
        ),
        out_shape=[jax.ShapeDtypeStruct(s, BF) for s in shapes],
        name="rounded",
    )(zl[None], weight, weight)


def place_kernel(at, *refs):
    out = refs[-1]
    n = refs[0].shape[1]
    for j, q in enumerate(refs[:-1]):
        out[:, pl.ds(pl.multiple_of(at[j] * n, n), n)] = q[...].astype(F32)


def place(at, parts):
    rows, n = parts[0].shape
    return pl.pallas_call(
        place_kernel,
        grid_spec=pltpu.PrefetchScalarGridSpec(
            num_scalar_prefetch=1,
            grid=(1,),
            in_specs=[pl.BlockSpec((rows, n), lambda i, at: (0, 0))] * len(parts),
            out_specs=pl.BlockSpec((rows, n * len(parts)), lambda i, at: (0, 0)),
        ),
        out_shape=jax.ShapeDtypeStruct((rows, n * len(parts)), F32),
        name="place",
    )(at, *parts)


def grad_kernel(slope, w, *refs):
    total = jnp.dot(slope[...], w[...], preferred_element_type=F32)
    if len(refs) > 1:
        total += refs[0][...]
    refs[-1][...] = total


def token_grad(part, slope, w, others=()):
    m, n = slope.shape[0] // 2, slope.shape[1]
    d = w.shape[1]
    cols = 256
    return pl.pallas_call(
        grad_kernel,
        grid=(d // cols,),
        in_specs=[
            pl.BlockSpec((m, n), lambda i: (part, 0)),
            pl.BlockSpec((n, cols), lambda i: (0, i)),
            *([pl.BlockSpec((m, cols), lambda i: (0, i))] * len(others)),
        ],
        out_specs=pl.BlockSpec((m, cols), lambda i: (0, i)),
        out_shape=jax.ShapeDtypeStruct((m, d), F32),
        compiler_params=pltpu.CompilerParams(vmem_limit_bytes=56 * 1024 * 1024),
        cost_estimate=pl.CostEstimate(flops=2 * m * n * d, bytes_accessed=2 * n * d + 8 * m * d, transcendentals=0),
        name=f"token_grad_{part}",
    )(slope, w, *others)


def copy_kernel(at, src, *refs):
    refs[-1][...] = src[...]


def unpack(act, received, c, rows):
    m, n = act.shape
    return pl.pallas_call(
        copy_kernel,
        grid_spec=pltpu.PrefetchScalarGridSpec(
            num_scalar_prefetch=1,
            grid=(n // rows // 2,),
            in_specs=[pl.BlockSpec((m, rows), lambda i, at: (0, i)), pl.BlockSpec(memory_space=pl.ANY)],
            out_specs=pl.BlockSpec((m, rows), lambda i, at: (0, 2 * i + 1 - at[0])),
        ),
        out_shape=jax.ShapeDtypeStruct((m, n), BF),
        input_output_aliases={2: 0},
        name="unpack",
    )(c[None], received, act)


def local(tokens, weight, cotangent):
    rows = weight.shape[0]
    m = tokens.shape[0]
    f, r = lax.axis_index("fsdp"), lax.axis_index("rep")
    x, y, zh, zl, c = coords(f, r)
    total_tokens = m * lax.axis_size("fsdp") * lax.axis_size("rep")
    scale = 1.0 / math.sqrt(total_tokens)

    xa = jnp.where(c == 0, x ^ 1, 3 - x)
    xb = jnp.where(c == 0, 3 - x, x ^ 1)
    at_x = {"own": x, "a": xa, "b": xb, "ab": (x + 2) % 4}
    y0, y1 = y % 2, y // 2
    y_half = jnp.where(c == 0, y0 ^ y1, y1)
    y_part = jnp.where(c == 0, y1, y0)
    at = []
    for name in ROLES:
        there = 2 * at_x[name.removesuffix("_z")] + (1 - zh if name.endswith("_z") else zh)
        at += [2 * there + c, there, y_half, zl, y_part]
    at = jnp.stack(at).astype(jnp.int32).reshape(len(ROLES), -1)

    bufs = ()
    keep, got, got_q = {}, {}, {}

    def meet(*values):
        nonlocal at
        at, *values = lax.optimization_barrier((at, *values))
        return values

    def run(name, w, earlier=None):
        nonlocal bufs
        pair = (keep[earlier], got[earlier]) if earlier else ()
        bufs, send, keep[name], *q = block(
            ROLES.index(name), at, tokens, tok_p, w, cotangent, cot_p, pair, bufs, scale
        )
        return (send, *q)

    def part_of(v, part):
        n = v.shape[1] // 2
        return lax.dynamic_slice_in_dim(v, part * n, n, 1).astype(F32)

    def quarter_to_send(name):
        return (part_of(keep[name], 1 - y_part) + part_of(got[name], 1 - y_part)).astype(BF)

    def total(name, *others):
        terms = [part_of(keep[name], y_part), part_of(got[name], y_part), got_q[name].astype(F32)]
        return sum(terms + [v.astype(F32) for v in others]).astype(BF)

    tok_p = other_core(tokens)
    cot_p = other_core(cotangent)
    own_far, own_near, own = rounded(zl, weight)
    a_far = x_first(own_far)
    oz_near = z_outer(own_far)
    a_near = x_first(own_near)

    tok_p, cot_p, own = meet(tok_p, cot_p, own)
    b = x_second(own)
    (send,) = run("own", (own_far, own_near))

    send, a_far, a_near, oz_near = meet(send, a_far, a_near, oz_near)
    oz_far, az_near = z_inner(oz_near), z_outer(a_far)
    got["own"] = y_first(send)
    (send,) = run("a", (a_far, a_near))

    send, got["own"], b = meet(send, got["own"], b)
    got["a"] = y_first(send)
    ab = x_first(b)
    send, q = run("b", (b,), "own")

    send, q, got["a"], oz_far, az_near, b_far = meet(send, q, got["a"], oz_far, az_near, b[: rows // 2])
    az_far, bz_near = z_inner(az_near), z_outer(b_far)
    got["b"], got_q["own"] = y_first(send), y_second(q)
    send, q = run("own_z", (oz_far, oz_near), "a")

    send, q, ab, got["b"], got_q["own"], az_near = meet(send, q, ab, got["b"], got_q["own"], az_near)
    abz_near = x_second(az_near)
    got["own_z"], got_q["a"] = y_first(send), y_second(q)
    send, q = run("ab", (ab,), "b")

    send, q, got["own_z"], got_q["a"], abz_near, az_far, bz_near = meet(
        send, q, got["own_z"], got_q["a"], abz_near, az_far, bz_near
    )
    bz_far, abz_far = z_inner(bz_near), x_second(az_far)
    got["ab"], got_q["b"] = y_first(send), y_second(q)
    send, q = run("a_z", (az_far, az_near), "own_z")

    send, q, got["ab"], got_q["b"], abz_far = meet(send, q, got["ab"], got_q["b"], abz_far)
    got["a_z"], got_q["own_z"] = y_first(send), y_second(q)
    send, q = run("ab_z", (abz_far, abz_near), "ab")

    send, q, got["a_z"], got_q["own_z"], bz_far = meet(send, q, got["a_z"], got_q["own_z"], bz_far)
    got["ab_z"], got_q["ab"] = y_first(send), y_second(q)
    send, q = run("b_z", (bz_far, bz_near), "a_z")
    act, act_p, slope, w_all = bufs

    send, q, got["ab_z"], got_q["ab"], act_p, slope = meet(send, q, got["ab_z"], got_q["ab"], act_p, slope)
    got["b_z"], got_q["a_z"] = y_first(send), y_second(q)
    got_q["ab_z"] = y_second(quarter_to_send("ab_z"))
    got_x = x_first(jnp.concatenate([total("a"), total("ab")]))
    act_p = other_core(act_p)
    grad_p = token_grad(1, slope, w_all)

    grad_p, got["b_z"], got_q["a_z"], got_q["ab_z"], got_x, act_p, act = meet(
        grad_p, got["b_z"], got_q["a_z"], got_q["ab_z"], got_x, act_p, act
    )
    got_q["b_z"] = y_second(quarter_to_send("b_z"))
    got_x2 = x_second(total("b", got_x[rows:]))
    got_xz = x_first(jnp.concatenate([total("a_z"), total("ab_z")]))
    swapped = other_core(grad_p)
    activated = unpack(act, act_p, c, rows)

    activated, got_q["b_z"], got_x2, got_xz = meet(activated, got_q["b_z"], got_x2, got_xz)
    got_xz2 = x_second(total("b_z", got_xz[rows:]))
    same = total("own", got_x[:rows], got_x2)
    same_z = z_inner(same)

    got_xz2, same_z, swapped, slope = meet(got_xz2, same_z, swapped, slope)
    other = total("own_z", got_xz[:rows], got_xz2)
    z1, z2 = z_outer(other), z_across(other)
    input_grad = token_grad(0, slope, w_all, (swapped,))

    part = sum(v.astype(F32) for v in (same, same_z, z1, z2)).astype(BF)
    parts = [part, y_second(part), y_first(part)]
    parts.append(y_first(parts[1]))
    here = 2 * y_half + y_part
    across = 2 * (1 - y_half) + (y_part ^ c)
    weight_grad = place(jnp.stack([here, here ^ 1, across, across ^ 1]).astype(jnp.int32), parts)
    return activated, input_grad, weight_grad


def solution(mesh):
    in_specs = (P(("fsdp", "rep"), None), P("fsdp", None), P(("fsdp", "rep"), None))
    out_specs = (P(("fsdp", "rep"), None), P(("fsdp", "rep"), None), P("fsdp", None))
    return jax.shard_map(local, mesh=mesh, in_specs=in_specs, out_specs=out_specs, check_vma=False)
```

```python
import functools
import math

import jax
import jax.numpy as jnp
from jax import lax
from jax.experimental import pallas as pl
from jax.experimental.pallas import tpu as pltpu
from jax.sharding import PartitionSpec as P

BF = jnp.bfloat16
F32 = jnp.float32
NX, NY = 4, 4
TILE = 256
ROWS = 384
PARTS = {"whole": 1, "halves": 2, "quarters": 4}
SMALL = pl.CostEstimate(flops=1, bytes_accessed=1, transcendentals=0)
COST = pl.CostEstimate(flops=10**13, bytes_accessed=10**10, transcendentals=0)
ROLES = ("own", "a", "b", "ab", "a_z", "b_z", "ab_z", "own_z")


def coords(f, r):
    return f // 4, r // 2, (f // 2) % 2, r % 2, f % 2


def permute(value, target):
    pairs = []
    for i in range(128):
        x, y, zh, zl, c = target(*coords(i // 8, i % 8))
        pairs.append((i, (x * 4 + zh * 2 + c) * 8 + y * 2 + zl))
    return lax.ppermute(value, ("fsdp", "rep"), pairs)


def first(i, c):
    return i ^ 1 if c == 0 else 3 - i


def second(i, c):
    return first(i, 1 - c)


def x_first(v):
    return permute(v, lambda x, y, zh, zl, c: (first(x, c), y, zh, zl, c))


def x_second(v):
    return permute(v, lambda x, y, zh, zl, c: (second(x, c), y, zh, zl, c))


def x_across(v):
    return permute(v, lambda x, y, zh, zl, c: ((x + 2) % 4, y, zh, zl, c))


def y_first(v):
    return permute(v, lambda x, y, zh, zl, c: (x, first(y, c), zh, zl, c))


def y_second(v):
    return permute(v, lambda x, y, zh, zl, c: (x, second(y, c), zh, zl, c))


def y_across(v):
    return permute(v, lambda x, y, zh, zl, c: (x, (y + 2) % 4, zh, zl, c))


def z_outer(v):
    return permute(v, lambda x, y, zh, zl, c: (x, y, 1 - zh, 1 - zl, c))


def z_inner(v):
    return permute(v, lambda x, y, zh, zl, c: (x, y, zh, 1 - zl, c))


def z_across(v):
    return permute(v, lambda x, y, zh, zl, c: (x, y, 1 - zh, zl, c))


def other_core(v):
    return permute(v, lambda x, y, zh, zl, c: (x, y, zh, zl, 1 - c))


def gelu_and_slope(pre, cot):
    k = math.sqrt(2.0 / math.pi)
    square = pre * pre
    t = jnp.tanh(pre * (k + (k * 0.044715) * square))
    half = 0.5 + 0.5 * t
    act = pre * half
    slope = half + (act - act * t) * (k + (3 * k * 0.044715) * square)
    return act.astype(BF), (cot.astype(F32) * slope).astype(BF)


def block_kernel(first, kinds, scale, n_alias, folds, adds, at, tok_o, tok_p, *refs):
    n_sums, n_blocks = len(folds), len(kinds)
    w_in, refs = refs[:n_blocks], refs[n_blocks:]
    (cot_o, cot_p), refs = refs[:2], refs[2:]
    add_in, refs = refs[:adds], refs[adds:]
    earlier, refs = refs[: 2 * n_sums], refs[2 * n_sums + n_alias :]
    (act_o, act_p, slope_o, w_o), refs = refs[:4], refs[4:]
    part_o = []
    for kind in kinds:
        part_o.append(refs[: PARTS[kind]])
        refs = refs[PARTS[kind] :]
    quarter_o, refs = refs[: n_sums > 0], refs[n_sums > 0 :]
    (tok, cot, w, act, slope, halves, load_sem, store_sem), refs = refs[:8], refs[8:]
    add, refs = refs[:adds], refs[adds:]
    m, rows, width = tok.shape[1], w.shape[1], halves.shape[3]
    loads, stores = [], []

    def load(src, dst):
        copy = pltpu.make_async_copy(src, dst, load_sem.at[len(loads)])
        copy.start()
        loads.append(copy)
        return copy

    def store(src, dst):
        copy = pltpu.make_async_copy(src, dst, store_sem.at[len(stores)])
        copy.start()
        stores.append(copy)

    def cols(k, width):
        return pl.ds(pl.multiple_of(k * width, width), width)

    y_half, y_part, y_other = at[first, 1], at[first, 2], at[first, 3]
    tok_loads, w_loads, cot_loads = [], [], []
    for k in range(n_blocks):
        w_loads.append(load(w_in[k], w.at[k]))
        for j in range(2):
            if k == 0:
                tok_in = (tok_o, tok_p)[j]
                tok_loads.append([load(tok_in.at[s : s + TILE], tok.at[j, s : s + TILE]) for s in range(0, m, TILE)])
            cot_loads.append(load((cot_o, cot_p)[j].at[:, cols(at[first + k, 0], rows)], cot.at[k, j]))
    order = (1 - y_half, y_half)
    add_loads = [load(add_in[0].at[:, cols(h, width)], add[0].at[k]) for k, h in enumerate(order * adds)]
    q = width // 2
    q_loads = []
    for k in range(n_sums):
        rows_at = pl.ds(sum(folds[:k]), folds[k])
        for h in range(2):
            q_loads.append(load(earlier[2 * k + h].at[:, cols(1 - y_part, q)], refs[0].at[h, rows_at]))

    for k in range(n_blocks):
        role = first + k
        w_loads[k].wait()
        place = slice(role * rows, (role + 1) * rows)
        act_out = (act_o.at[:, cols(at[role, 0], rows)], act_p.at[:, place])
        store(w.at[k], w_o.at[place])
        for j in range(2):
            cot_loads[2 * k + j].wait()
            for t, s in enumerate(range(0, m, TILE)):
                if k == 0:
                    tok_loads[j][t].wait()
                r = slice(s, s + TILE)
                pre = lax.dot_general(tok[j, r], w[k], (((1,), (1,)), ((), ())), preferred_element_type=F32)
                act[k, j, r], slope[k, j * m + s : j * m + s + TILE] = gelu_and_slope(pre, cot[k, j, r])
            store(act.at[k, j], act_out[j])
            mine = slice(j * m, (j + 1) * m)
            store(slope.at[k, mine], slope_o.at[mine, place])
        if k == 0 and n_sums:
            for copy in q_loads:
                copy.wait()
            refs[1][...] = (refs[0][0].astype(F32) + refs[0][1].astype(F32)).astype(BF)
            store(refs[1], quarter_o[0])
        for copy in add_loads if k == 0 else ():
            copy.wait()
        for h, half in enumerate(order):
            mine = cols(half, width)
            both = jnp.concatenate([tok[0, :, mine], tok[1, :, mine]], axis=0)
            term = lax.dot_general(slope[k], both, (((0,), (0,)), ((), ())), preferred_element_type=F32) * scale
            if adds:
                term += add[0][h].astype(F32)
            halves[k, h] = term.astype(BF)
            out = part_o[k]
            if kinds[k] == "whole":
                store(halves.at[k, h], out[0].at[:, mine])
            elif kinds[k] == "halves":
                store(halves.at[k, h], out[h])
            else:
                part = y_part if h else y_other
                store(halves.at[k, h, :, cols(part, q)], out[0 if h else 2])
                store(halves.at[k, h, :, cols(1 - part, q)], out[1 if h else 3])
    for copy in stores:
        copy.wait()


def block(first, at, tok_o, tok_p, w, kinds, cot_o, cot_p, add, earlier, bufs, scale):
    m, d = tok_o.shape
    rows = w[0].shape[0]
    nb = len(w)
    n_all = cot_o.shape[1]
    folds = [pair[0].shape[0] for pair in earlier]
    quarter = (sum(folds), d // 4)
    shapes = [(m, n_all), (m, n_all // 2), (2 * m, n_all // 2), (n_all // 2, d)]
    for kind in kinds:
        shapes += [(rows, d // PARTS[kind])] * PARTS[kind]
    shapes += [quarter] * (len(folds) > 0)
    args = [tok_o, tok_p, *w, cot_o, cot_p, *add, *[v for pair in earlier for v in pair], *bufs]
    adds = len(add)
    n_stores = 5 * nb + sum(max(2, PARTS[kind]) for kind in kinds) + 1
    out = pl.pallas_call(
        functools.partial(block_kernel, first, kinds, scale, len(bufs), folds, adds),
        grid_spec=pltpu.PrefetchScalarGridSpec(
            num_scalar_prefetch=1,
            grid=(1,),
            in_specs=[pl.BlockSpec(memory_space=pl.ANY)] * len(args),
            out_specs=[pl.BlockSpec(memory_space=pl.ANY)] * len(shapes),
            scratch_shapes=[
                pltpu.VMEM((2, m, d), BF),
                pltpu.VMEM((nb, 2, m, rows), BF),
                pltpu.VMEM((nb, rows, d), BF),
                pltpu.VMEM((nb, 2, m, rows), BF),
                pltpu.VMEM((nb, 2 * m, rows), BF),
                pltpu.VMEM((nb, 2, rows, d // 2), BF),
                pltpu.SemaphoreType.DMA((3 * nb + 2 * (m // TILE) + 2 * adds + 2 * len(folds),)),
                pltpu.SemaphoreType.DMA((n_stores,)),
            ]
            + [pltpu.VMEM((2, rows, d // 2), BF)] * adds
            + [pltpu.VMEM((2, *quarter), BF), pltpu.VMEM(quarter, BF)] * (len(folds) > 0),
        ),
        out_shape=[jax.ShapeDtypeStruct(s, BF) for s in shapes],
        input_output_aliases={1 + len(args) - len(bufs) + j: j for j in range(len(bufs))},
        compiler_params=pltpu.CompilerParams(vmem_limit_bytes=56 * 1024 * 1024),
        cost_estimate=COST,
        name=f"block_{first}",
    )(at, *args)
    return out[:4], *out[4:]


def place_kernel(n_parts, at, *refs):
    parts, out, (held, sems) = refs[:n_parts], refs[-3], refs[-2:]
    n = parts[0].shape[1]
    copies = []
    for j, part in enumerate(parts):
        held[j] = part[...].astype(F32)
        target = out.at[:, pl.ds(pl.multiple_of(at[j] * n, n), n)]
        copies.append(pltpu.make_async_copy(held.at[j], target, sems.at[j]))
        copies[-1].start()
    for copy in copies:
        copy.wait()


def place(at, parts, base=None):
    rows, n = parts[0].shape
    anywhere = pl.BlockSpec(memory_space=pl.ANY)
    some = base is not None
    return pl.pallas_call(
        functools.partial(place_kernel, len(parts)),
        grid_spec=pltpu.PrefetchScalarGridSpec(
            num_scalar_prefetch=1,
            grid=(1,),
            in_specs=[pl.BlockSpec((rows, n), lambda i, at: (0, 0))] * len(parts) + [anywhere] * some,
            out_specs=anywhere,
            scratch_shapes=[pltpu.VMEM((len(parts), rows, n), F32), pltpu.SemaphoreType.DMA((len(parts),))],
        ),
        out_shape=jax.ShapeDtypeStruct((rows, 4 * n), F32),
        input_output_aliases={1 + len(parts): 0} if some else {},
        compiler_params=pltpu.CompilerParams(vmem_limit_bytes=56 * 1024 * 1024),
        cost_estimate=COST,
        name="place",
    )(at, *parts, *([base] * some))


def grad_kernel(slope, w, *refs):
    total = jnp.dot(slope[...], w[...], preferred_element_type=F32)
    for term in refs[:-1]:
        total += term[...]
    refs[-1][...] = total


def token_grad(part, slope, w, terms=(), half=None):
    m, n = slope.shape[0] // 2, slope.shape[1]
    d = w.shape[1]
    cols = 512
    depth, k = (n, 0) if half is None else (n // 2, half)
    tile = pl.BlockSpec((m, cols), lambda i: (0, i))
    return pl.pallas_call(
        grad_kernel,
        grid=(d // cols,),
        in_specs=[
            pl.BlockSpec((m, depth), lambda i: (part, k)),
            pl.BlockSpec((depth, cols), lambda i: (k, i)),
            *([tile] * len(terms)),
        ],
        out_specs=tile,
        out_shape=jax.ShapeDtypeStruct((m, d), F32),
        compiler_params=pltpu.CompilerParams(vmem_limit_bytes=56 * 1024 * 1024),
        cost_estimate=SMALL,
        name=f"token_grad_{part}",
    )(slope, w, *terms)


def finish_kernel(at, mine, other, *refs):
    i = pl.program_id(0)
    parts, _, out, act, held, sems = refs
    rows = held.shape[2]
    count = held.shape[0]

    def read(k):
        part = parts.at[:, k * rows : (k + 1) * rows]
        return pltpu.make_async_copy(part, held.at[k], sems.at[0, k])

    def write(k):
        target = act.at[:, pl.ds(pl.multiple_of(at[k] * rows, rows), rows)]
        return pltpu.make_async_copy(held.at[k], target, sems.at[1, k])

    @pl.when(i == 0)
    def _():
        for k in range(count):
            read(k).start()

    out[...] = mine[...] + other[...]

    @pl.when(i == 1)
    def _():
        for k in range(count):
            read(k).wait()
            write(k).start()

    @pl.when(i == pl.num_programs(0) - 1)
    def _():
        for k in range(count):
            write(k).wait()


def finish(at, mine, other, act, parts):
    m, d = mine.shape
    rows = ROWS
    tile = pl.BlockSpec((m // 4, d), lambda i, at: (i, 0))
    anywhere = pl.BlockSpec(memory_space=pl.ANY)
    count = parts.shape[1] // rows
    return pl.pallas_call(
        finish_kernel,
        grid_spec=pltpu.PrefetchScalarGridSpec(
            num_scalar_prefetch=1,
            grid=(4,),
            in_specs=[tile, tile] + [anywhere] * 2,
            out_specs=[tile, anywhere],
            scratch_shapes=[pltpu.VMEM((count, m, rows), BF), pltpu.SemaphoreType.DMA((2, count))],
        ),
        out_shape=[jax.ShapeDtypeStruct((m, d), F32), jax.ShapeDtypeStruct(act.shape, BF)],
        input_output_aliases={4: 1},
        compiler_params=pltpu.CompilerParams(vmem_limit_bytes=56 * 1024 * 1024),
        cost_estimate=SMALL,
        name="finish",
    )(at, mine, other, parts, act)


def local(tokens, weight, cotangent):
    m = tokens.shape[0]
    f, r = lax.axis_index("fsdp"), lax.axis_index("rep")
    x, y, zh, zl, c = coords(f, r)
    total_tokens = m * lax.axis_size("fsdp") * lax.axis_size("rep")
    scale = 1.0 / math.sqrt(total_tokens)

    y0, y1 = y % 2, y // 2
    y_half = jnp.where(c == 0, y0 ^ y1, y1)
    y_part = jnp.where(c == 0, y1, y0)

    def columns(c):
        xa = jnp.where(c == 0, x ^ 1, 3 - x)
        xb = jnp.where(c == 0, 3 - x, x ^ 1)
        at_x = {"own": x, "a": xa, "b": xb, "ab": (x + 2) % 4}
        return [
            4 * at_x[name.removesuffix("_z")] + 2 * (1 - zh if name.endswith("_z") else zh) + c for name in ROLES
        ]

    at = jnp.stack([v for col in columns(c) for v in (col, y_half, y_part, y_part ^ c)]).astype(jnp.int32).reshape(len(ROLES), -1)
    at_other = jnp.stack(columns(1 - c)).astype(jnp.int32)
    at_part = jnp.stack([y_part, 1 - y_part]).astype(jnp.int32)

    bufs = ()
    keep, got, got_q = {}, {}, {}

    def meet(*values):
        nonlocal at
        at, *values = lax.optimization_barrier((at, *values))
        return values

    def run(name, *w, fold=(), add=(), kinds=None):
        nonlocal bufs
        first = ROLES.index(name)
        pairs = [(keep[k], got[k]) for k in fold]
        kinds = kinds or ("halves",) * len(w)
        bufs, *out = block(first, at, tokens, tok_p, w, kinds, cotangent, cot_p, add, pairs, bufs, scale)
        return out

    def quarter_to_send(name):
        return [(keep[name], 0, 1), (got[name], 0, 1)]

    def total(name, *others):
        return [(keep[name], 0, 0), (got[name], 0, 0), got_q[name], *others]

    def only(total, *more):
        def one(terms):
            value = 0.0
            for v, row, col in terms:
                v = v[row * ROWS : (row + 1) * ROWS]
                if col is not None:
                    v = lax.dynamic_slice_in_dim(v, at_part[col] * (v.shape[1] // 2), v.shape[1] // 2, 1)
                value += v.astype(F32)
            return value.astype(BF)

        return jnp.concatenate([one(terms) for terms in (total, *more)]) if more else one(total)

    tok_p = other_core(tokens)
    cot_p = other_core(cotangent)
    own = weight.astype(BF)
    a = x_first(own)
    oz = z_outer(own)

    tok_p, cot_p, own = meet(tok_p, cot_p, own)
    b = x_second(own)
    send, keep["own"] = run("own", own)

    send, a = meet(send, a)
    got["own"], az = y_first(send), z_outer(a)
    send, keep["a"] = run("a", a)

    send, b, got["own"] = meet(send, b, got["own"])
    got["a"], ab = y_first(send), x_first(b)
    send, keep["b"] = run("b", b)

    send, ab, got["a"], oz = meet(send, ab, got["a"], oz)
    got["b"], bz = y_first(send), x_second(oz)
    send, keep["ab"], q = run("ab", ab, fold=("own", "a"))

    send, q, got["b"], slope, w_all = meet(send, q, got["b"], *bufs[2:])
    bufs = [*bufs[:2], slope, w_all]
    got["ab"] = y_first(send)
    grad_o = token_grad(0, slope, w_all, half=0)
    grad_o, az, bz, got["ab"], q = meet(grad_o, az, bz, got["ab"], q)
    abz, got_two = x_second(az), y_second(q)
    whole, send, keep["b_z"], q = run("a_z", az, bz, fold=("b", "ab"), kinds=("whole", "halves"))

    whole, send, q, abz, got_two = meet(whole, send, q, abz, got_two)
    got_q["own"], got_q["a"] = (got_two, 0, None), (got_two, 1, None)
    got["b_z"], whole, got_two = y_first(send), x_first(whole), y_second(q)
    abz_parts = run("ab_z", abz, kinds=("quarters",))

    *abz_parts, got["b_z"] = meet(*abz_parts, got["b_z"])
    got_abz = [y_second(abz_parts[1]), y_first(abz_parts[2]), y_across(abz_parts[3])]
    got_bz = y_second(only(quarter_to_send("b_z")))
    (whole,) = meet(whole)
    oz_parts = run("own_z", oz, add=(whole,), kinds=("quarters",))
    act, act_p, slope, w_all = bufs

    *oz_parts, slope, got_two = meet(*oz_parts, slope, got_two)
    got_q["b"], got_q["ab"] = (got_two, 0, None), (got_two, 1, None)
    got_x = x_second(only(total("b"), total("ab")))
    grad_p = token_grad(1, slope, w_all)

    *oz_parts, grad_p, got_x, got_bz, g1, g2, g3 = meet(*oz_parts, grad_p, got_x, got_bz, *got_abz)
    got_oz = [y_second(oz_parts[1]), y_first(oz_parts[2]), y_across(oz_parts[3])]
    got_q["b_z"] = (got_bz, 0, None)
    got_x2 = x_across(only([(v, 0, None) for v in (abz_parts[0], g1, g2, g3)]))
    got_x3 = x_second(only(total("b_z")))
    got_x1 = x_first(only(total("a", (got_x, 1, None))))
    grad_o = token_grad(0, slope, w_all, (grad_o,), half=1)

    *got_oz, got_x1, got_x2, got_x3, grad_o, grad_p, act_p = meet(*got_oz, got_x1, got_x2, got_x3, grad_o, grad_p, act_p)
    other = only([(v, 0, None) for v in (oz_parts[0], *got_oz, got_x2, got_x3)])
    z1, z2 = z_outer(other), z_across(other)
    same = only(total("own", (got_x, 0, None), (got_x1, 0, None)))
    same_z = z_inner(same)
    swapped, act_p = other_core(grad_p), other_core(act_p)
    input_grad, activated = finish(at_other, grad_o, swapped, act, act_p)

    z1, z2, same_z, input_grad = meet(z1, z2, same_z, input_grad)

    part = sum(v.astype(F32) for v in (same, same_z, z1, z2)).astype(BF)
    here = 2 * y_half + y_part
    across = 2 * (1 - y_half) + (y_part ^ c)
    second_part, first_part = meet(y_second(part), y_first(part))
    last_part = y_first(second_part)
    weight_grad = place(jnp.stack([here, here ^ 1, across]).astype(jnp.int32), [part, second_part, first_part])
    weight_grad, last_part = meet(weight_grad, last_part)
    weight_grad = place((across ^ 1)[None].astype(jnp.int32), [last_part], weight_grad)
    return activated, input_grad, weight_grad


def solution(mesh):
    in_specs = (P(("fsdp", "rep"), None), P("fsdp", None), P(("fsdp", "rep"), None))
    out_specs = (P(("fsdp", "rep"), None), P(("fsdp", "rep"), None), P("fsdp", None))
    return jax.shard_map(local, mesh=mesh, in_specs=in_specs, out_specs=out_specs, check_vma=False)
```

```python
import functools
import math

import jax
import jax.numpy as jnp
from jax import lax
from jax.experimental import pallas as pl
from jax.experimental.pallas import tpu as pltpu
from jax.sharding import PartitionSpec as P

BF = jnp.bfloat16
F32 = jnp.float32
NX, NY = 4, 4
TILE = 512
ROWS = 384
PARTS = {"whole": 1, "halves": 2, "quarters": 4}
SMALL = pl.CostEstimate(flops=1, bytes_accessed=1, transcendentals=0)
COST = pl.CostEstimate(flops=10**13, bytes_accessed=10**10, transcendentals=0)
ROLES = ("own", "a", "b", "ab", "a_z", "b_z", "ab_z", "own_z")


def coords(f, r):
    return f // 4, r // 2, (f // 2) % 2, r % 2, f % 2


def permute(value, target):
    pairs = []
    for i in range(128):
        x, y, zh, zl, c = target(*coords(i // 8, i % 8))
        pairs.append((i, (x * 4 + zh * 2 + c) * 8 + y * 2 + zl))
    return lax.ppermute(value, ("fsdp", "rep"), pairs)


def first(i, c):
    return i ^ 1 if c == 0 else 3 - i


def second(i, c):
    return first(i, 1 - c)


def x_first(v):
    return permute(v, lambda x, y, zh, zl, c: (first(x, c), y, zh, zl, c))


def x_second(v):
    return permute(v, lambda x, y, zh, zl, c: (second(x, c), y, zh, zl, c))


def x_across(v):
    return permute(v, lambda x, y, zh, zl, c: ((x + 2) % 4, y, zh, zl, c))


def y_first(v):
    return permute(v, lambda x, y, zh, zl, c: (x, first(y, c), zh, zl, c))


def y_second(v):
    return permute(v, lambda x, y, zh, zl, c: (x, second(y, c), zh, zl, c))


def y_across(v):
    return permute(v, lambda x, y, zh, zl, c: (x, (y + 2) % 4, zh, zl, c))


def z_outer(v):
    return permute(v, lambda x, y, zh, zl, c: (x, y, 1 - zh, 1 - zl, c))


def z_inner(v):
    return permute(v, lambda x, y, zh, zl, c: (x, y, zh, 1 - zl, c))


def z_across(v):
    return permute(v, lambda x, y, zh, zl, c: (x, y, 1 - zh, zl, c))


def other_core(v):
    return permute(v, lambda x, y, zh, zl, c: (x, y, zh, zl, 1 - c))


def gelu_and_slope(pre, cot):
    k = math.sqrt(2.0 / math.pi)
    square = pre * pre
    t = jnp.tanh(pre * (k + (k * 0.044715) * square))
    half = 0.5 + 0.5 * t
    act = pre * half
    slope = half + (act - act * t) * (k + (3 * k * 0.044715) * square)
    return act.astype(BF), (cot.astype(F32) * slope).astype(BF)


def block_kernel(first, n_blocks, kind, scale, n_alias, folds, adds, at, tok_o, tok_p, *refs):
    n_sums = len(folds)
    w_in, refs = refs[:n_blocks], refs[n_blocks:]
    (cot_o, cot_p), refs = refs[:2], refs[2:]
    add_in, refs = refs[:adds], refs[adds:]
    earlier, refs = refs[: 2 * n_sums], refs[2 * n_sums + n_alias :]
    (act_o, act_p, slope_o, w_o), refs = refs[:4], refs[4:]
    part_o, refs = refs[: PARTS[kind]], refs[PARTS[kind] :]
    quarter_o, refs = refs[: n_sums > 0], refs[n_sums > 0 :]
    (tok, cot, w, act, slope, halves, load_sem, store_sem), refs = refs[:8], refs[8:]
    add, refs = refs[:adds], refs[adds:]
    m, rows, width = tok.shape[1], w.shape[1], halves.shape[3]
    loads, stores = [], []

    def load(src, dst):
        copy = pltpu.make_async_copy(src, dst, load_sem.at[len(loads)])
        copy.start()
        loads.append(copy)
        return copy

    def store(src, dst):
        copy = pltpu.make_async_copy(src, dst, store_sem.at[len(stores)])
        copy.start()
        stores.append(copy)

    def cols(k, width):
        return pl.ds(pl.multiple_of(k * width, width), width)

    y_half, y_part, y_other = at[first, 1], at[first, 2], at[first, 3]
    tok_loads, w_loads, cot_loads = [], [], []
    for k in range(n_blocks):
        w_loads.append(load(w_in[k], w.at[k]))
        for j in range(2):
            if k == 0:
                tok_in = (tok_o, tok_p)[j]
                tok_loads.append([load(tok_in.at[s : s + TILE], tok.at[j, s : s + TILE]) for s in range(0, m, TILE)])
            cot_loads.append(load((cot_o, cot_p)[j].at[:, cols(at[first + k, 0], rows)], cot.at[k, j]))
    order = (1 - y_half, y_half)
    add_loads = [load(add_in[0].at[:, cols(h, width)], add[0].at[k]) for k, h in enumerate(order * adds)]
    q = width // 2
    q_loads = []
    for k in range(n_sums):
        rows_at = pl.ds(sum(folds[:k]), folds[k])
        for h in range(2):
            q_loads.append(load(earlier[2 * k + h].at[:, cols(1 - y_part, q)], refs[0].at[h, rows_at]))

    for k in range(n_blocks):
        role = first + k
        w_loads[k].wait()
        place = slice(role * rows, (role + 1) * rows)
        act_out = (act_o.at[:, cols(at[role, 0], rows)], act_p.at[:, place])
        store(w.at[k], w_o.at[place])
        for j in range(2):
            cot_loads[2 * k + j].wait()
            for t, s in enumerate(range(0, m, TILE)):
                if k == 0:
                    tok_loads[j][t].wait()
                r = slice(s, s + TILE)
                pre = lax.dot_general(tok[j, r], w[k], (((1,), (1,)), ((), ())), preferred_element_type=F32)
                act[k, j, r], slope[k, j * m + s : j * m + s + TILE] = gelu_and_slope(pre, cot[k, j, r])
            store(act.at[k, j], act_out[j])
            mine = slice(j * m, (j + 1) * m)
            store(slope.at[k, mine], slope_o.at[mine, place])
        if k == 0 and n_sums:
            for copy in q_loads:
                copy.wait()
            refs[1][...] = (refs[0][0].astype(F32) + refs[0][1].astype(F32)).astype(BF)
            store(refs[1], quarter_o[0])
        for copy in add_loads if k == 0 else ():
            copy.wait()
        for h, half in enumerate(order):
            mine = cols(half, width)
            both = jnp.concatenate([tok[0, :, mine], tok[1, :, mine]], axis=0)
            term = lax.dot_general(slope[k], both, (((0,), (0,)), ((), ())), preferred_element_type=F32) * scale
            if adds:
                term += add[0][h].astype(F32)
            halves[k, h] = term.astype(BF)
            mine_rows = slice(k * rows, (k + 1) * rows)
            out = [v.at[mine_rows] for v in part_o]
            if kind == "whole":
                store(halves.at[k, h], out[0].at[:, mine])
            elif kind == "halves":
                store(halves.at[k, h], out[h])
            else:
                part = y_part if h else y_other
                store(halves.at[k, h, :, cols(part, q)], out[0 if h else 2])
                store(halves.at[k, h, :, cols(1 - part, q)], out[1 if h else 3])
    for copy in stores:
        copy.wait()


def block(first, at, tok_o, tok_p, w, kind, cot_o, cot_p, add, earlier, bufs, scale):
    m, d = tok_o.shape
    rows = w[0].shape[0]
    nb = len(w)
    n_all = cot_o.shape[1]
    folds = [pair[0].shape[0] for pair in earlier]
    quarter = (sum(folds), d // 4)
    shapes = [(m, n_all), (m, n_all // 2), (2 * m, n_all // 2), (n_all // 2, d)]
    shapes += [(nb * rows, d // PARTS[kind])] * PARTS[kind]
    shapes += [quarter] * (len(folds) > 0)
    args = [tok_o, tok_p, *w, cot_o, cot_p, *add, *[v for pair in earlier for v in pair], *bufs]
    adds = len(add)
    n_stores = 5 * nb + nb * max(2, PARTS[kind]) + 1
    out = pl.pallas_call(
        functools.partial(block_kernel, first, nb, kind, scale, len(bufs), folds, adds),
        grid_spec=pltpu.PrefetchScalarGridSpec(
            num_scalar_prefetch=1,
            grid=(1,),
            in_specs=[pl.BlockSpec(memory_space=pl.ANY)] * len(args),
            out_specs=[pl.BlockSpec(memory_space=pl.ANY)] * len(shapes),
            scratch_shapes=[
                pltpu.VMEM((2, m, d), BF),
                pltpu.VMEM((nb, 2, m, rows), BF),
                pltpu.VMEM((nb, rows, d), BF),
                pltpu.VMEM((nb, 2, m, rows), BF),
                pltpu.VMEM((nb, 2 * m, rows), BF),
                pltpu.VMEM((nb, 2, rows, d // 2), BF),
                pltpu.SemaphoreType.DMA((3 * nb + 2 * (m // TILE) + 2 * adds + 2 * len(folds),)),
                pltpu.SemaphoreType.DMA((n_stores,)),
            ]
            + [pltpu.VMEM((2, rows, d // 2), BF)] * adds
            + [pltpu.VMEM((2, *quarter), BF), pltpu.VMEM(quarter, BF)] * (len(folds) > 0),
        ),
        out_shape=[jax.ShapeDtypeStruct(s, BF) for s in shapes],
        input_output_aliases={1 + len(args) - len(bufs) + j: j for j in range(len(bufs))},
        compiler_params=pltpu.CompilerParams(vmem_limit_bytes=56 * 1024 * 1024),
        cost_estimate=COST,
        name=f"block_{first}",
    )(at, *args)
    return out[:4], *out[4:]


def place_kernel(n_parts, at, *refs):
    parts, out, (held, sems) = refs[:n_parts], refs[-3], refs[-2:]
    n = parts[0].shape[1]
    copies = []
    for j, part in enumerate(parts):
        held[j] = part[...].astype(F32)
        target = out.at[:, pl.ds(pl.multiple_of(at[j] * n, n), n)]
        copies.append(pltpu.make_async_copy(held.at[j], target, sems.at[j]))
        copies[-1].start()
    for copy in copies:
        copy.wait()


def place(at, parts, base=None):
    rows, n = parts[0].shape
    anywhere = pl.BlockSpec(memory_space=pl.ANY)
    some = base is not None
    return pl.pallas_call(
        functools.partial(place_kernel, len(parts)),
        grid_spec=pltpu.PrefetchScalarGridSpec(
            num_scalar_prefetch=1,
            grid=(1,),
            in_specs=[pl.BlockSpec((rows, n), lambda i, at: (0, 0))] * len(parts) + [anywhere] * some,
            out_specs=anywhere,
            scratch_shapes=[pltpu.VMEM((len(parts), rows, n), F32), pltpu.SemaphoreType.DMA((len(parts),))],
        ),
        out_shape=jax.ShapeDtypeStruct((rows, 4 * n), F32),
        input_output_aliases={1 + len(parts): 0} if some else {},
        compiler_params=pltpu.CompilerParams(vmem_limit_bytes=56 * 1024 * 1024),
        cost_estimate=COST,
        name="place",
    )(at, *parts, *([base] * some))


def grad_kernel(slope, w, *refs):
    total = jnp.dot(slope[...], w[...], preferred_element_type=F32)
    for term in refs[:-1]:
        total += term[...]
    refs[-1][...] = total


def token_grad(part, slope, w, terms=(), half=None):
    m, n = slope.shape[0] // 2, slope.shape[1]
    d = w.shape[1]
    cols = 512
    depth, k = (n, 0) if half is None else (n // 2, half)
    tile = pl.BlockSpec((m, cols), lambda i: (0, i))
    return pl.pallas_call(
        grad_kernel,
        grid=(d // cols,),
        in_specs=[
            pl.BlockSpec((m, depth), lambda i: (part, k)),
            pl.BlockSpec((depth, cols), lambda i: (k, i)),
            *([tile] * len(terms)),
        ],
        out_specs=tile,
        out_shape=jax.ShapeDtypeStruct((m, d), F32),
        compiler_params=pltpu.CompilerParams(vmem_limit_bytes=56 * 1024 * 1024),
        cost_estimate=SMALL,
        name=f"token_grad_{part}",
    )(slope, w, *terms)


def finish_kernel(at, mine, other, *refs):
    i = pl.program_id(0)
    parts, _, out, act, held, sems = refs
    rows = held.shape[2]
    count = held.shape[0]

    def read(k):
        part = parts.at[:, k * rows : (k + 1) * rows]
        return pltpu.make_async_copy(part, held.at[k], sems.at[0, k])

    def write(k):
        target = act.at[:, pl.ds(pl.multiple_of(at[k] * rows, rows), rows)]
        return pltpu.make_async_copy(held.at[k], target, sems.at[1, k])

    @pl.when(i == 0)
    def _():
        for k in range(count):
            read(k).start()

    out[...] = mine[...] + other[...]

    @pl.when(i == 1)
    def _():
        for k in range(count):
            read(k).wait()
            write(k).start()

    @pl.when(i == pl.num_programs(0) - 1)
    def _():
        for k in range(count):
            write(k).wait()


def finish(at, mine, other, act, parts):
    m, d = mine.shape
    rows = ROWS
    tile = pl.BlockSpec((m // 4, d), lambda i, at: (i, 0))
    anywhere = pl.BlockSpec(memory_space=pl.ANY)
    count = parts.shape[1] // rows
    return pl.pallas_call(
        finish_kernel,
        grid_spec=pltpu.PrefetchScalarGridSpec(
            num_scalar_prefetch=1,
            grid=(4,),
            in_specs=[tile, tile] + [anywhere] * 2,
            out_specs=[tile, anywhere],
            scratch_shapes=[pltpu.VMEM((count, m, rows), BF), pltpu.SemaphoreType.DMA((2, count))],
        ),
        out_shape=[jax.ShapeDtypeStruct((m, d), F32), jax.ShapeDtypeStruct(act.shape, BF)],
        input_output_aliases={4: 1},
        compiler_params=pltpu.CompilerParams(vmem_limit_bytes=56 * 1024 * 1024),
        cost_estimate=SMALL,
        name="finish",
    )(at, mine, other, parts, act)


def local(tokens, weight, cotangent):
    m = tokens.shape[0]
    f, r = lax.axis_index("fsdp"), lax.axis_index("rep")
    x, y, zh, zl, c = coords(f, r)
    total_tokens = m * lax.axis_size("fsdp") * lax.axis_size("rep")
    scale = 1.0 / math.sqrt(total_tokens)

    y0, y1 = y % 2, y // 2
    y_half = jnp.where(c == 0, y0 ^ y1, y1)
    y_part = jnp.where(c == 0, y1, y0)

    def columns(c):
        xa = jnp.where(c == 0, x ^ 1, 3 - x)
        xb = jnp.where(c == 0, 3 - x, x ^ 1)
        at_x = {"own": x, "a": xa, "b": xb, "ab": (x + 2) % 4}
        return [
            4 * at_x[name.removesuffix("_z")] + 2 * (1 - zh if name.endswith("_z") else zh) + c for name in ROLES
        ]

    at = jnp.stack([v for col in columns(c) for v in (col, y_half, y_part, y_part ^ c)]).astype(jnp.int32).reshape(len(ROLES), -1)
    at_other = jnp.stack(columns(1 - c)).astype(jnp.int32)
    at_part = jnp.stack([y_part, 1 - y_part]).astype(jnp.int32)

    bufs = ()
    keep, got, got_q = {}, {}, {}

    def meet(*values):
        nonlocal at
        at, *values = lax.optimization_barrier((at, *values))
        return values

    def run(name, *w, fold=(), add=(), kind="halves"):
        nonlocal bufs
        first = ROLES.index(name)
        pairs = [(keep[k], got[k]) for k in fold]
        bufs, *out = block(first, at, tokens, tok_p, w, kind, cotangent, cot_p, add, pairs, bufs, scale)
        return out

    def quarter_to_send(name, row=0):
        return [(keep[name], row, 1), (got[name], row, 1)]

    def total(name, *others, row=0):
        return [(keep[name], row, 0), (got[name], row, 0), got_q[name], *others]

    def only(total, *more):
        def one(terms):
            value = 0.0
            for v, row, col in terms:
                v = v[row * ROWS : (row + 1) * ROWS]
                if col is not None:
                    v = lax.dynamic_slice_in_dim(v, at_part[col] * (v.shape[1] // 2), v.shape[1] // 2, 1)
                value += v.astype(F32)
            return value.astype(BF)

        return jnp.concatenate([one(terms) for terms in (total, *more)]) if more else one(total)

    tok_p = other_core(tokens)
    cot_p = other_core(cotangent)
    own = weight.astype(BF)
    a = x_first(own)
    oz = z_outer(own)

    tok_p, cot_p, own = meet(tok_p, cot_p, own)
    b = x_second(own)
    send, keep["own"] = run("own", own)

    send, a = meet(send, a)
    got["own"], az = y_first(send), z_outer(a)
    send, keep["a"] = run("a", a)

    send, b, got["own"] = meet(send, b, got["own"])
    got["a"], ab = y_first(send), x_first(b)
    send, keep["b"] = run("b", b)

    send, ab, got["a"], oz = meet(send, ab, got["a"], oz)
    got["b"], bz = y_first(send), x_second(oz)
    send, keep["ab"], q = run("ab", ab, fold=("own", "a"))

    send, q, got["b"], az = meet(send, q, got["b"], az)
    got["ab"], got_two, abz = y_first(send), y_second(q), x_second(az)
    (whole,) = run("a_z", az, kind="whole")

    slope, w_all, whole, got["ab"], got_two, bz = meet(*bufs[2:], whole, got["ab"], got_two, bz)
    bufs = [*bufs[:2], slope, w_all]
    got_q["own"], got_q["a"] = (got_two, 0, None), (got_two, 1, None)
    got_two = y_second(only(quarter_to_send("b"), quarter_to_send("ab")))
    grad_o = token_grad(0, slope, w_all, half=0)

    grad_o, whole, abz = meet(grad_o, whole, abz)
    whole = x_first(whole)
    parts = run("b_z", bz, abz, kind="quarters")

    *parts, got_two = meet(*parts, got_two)
    got_q["b"], got_q["ab"] = (got_two, 0, None), (got_two, 1, None)
    parts = [parts[0], y_second(parts[1]), y_first(parts[2]), y_across(parts[3])]
    got_x = x_second(only(total("b"), total("ab")))
    send, keep["own_z"] = run("own_z", oz, add=(whole,))
    act, act_p, slope, w_all = bufs

    send, slope, got_x = meet(send, slope, got_x)
    got["own_z"] = y_first(send)
    grad_p = token_grad(1, slope, w_all)

    *parts, grad_p, got_x, act_p = meet(*parts, grad_p, got_x, act_p)
    got_x2, got_x3 = (
        permuted(only([(v, row, None) for v in parts])) for row, permuted in enumerate((x_second, x_across))
    )
    got_q["own_z"] = (y_second(only(quarter_to_send("own_z"))), 0, None)
    got_x1 = x_first(only(total("a", (got_x, 1, None))))
    swapped = other_core(grad_p)
    grad_o = token_grad(0, slope, w_all, (grad_o,), half=1)

    got_x1, got_x2, got_x3, got_oz, grad_o, swapped, act_p = meet(
        got_x1, got_x2, got_x3, got_q["own_z"][0], grad_o, swapped, act_p
    )
    got_q["own_z"] = (got_oz, 0, None)
    other = only(total("own_z", (got_x2, 0, None), (got_x3, 0, None)))
    z1, z2 = z_outer(other), z_across(other)
    same = only(total("own", (got_x, 0, None), (got_x1, 0, None)))
    same_z = z_inner(same)
    act_p = other_core(act_p)
    input_grad, activated = finish(at_other, grad_o, swapped, act, act_p)

    z1, z2, same_z, input_grad = meet(z1, z2, same_z, input_grad)

    part = sum(v.astype(F32) for v in (same, same_z, z1, z2)).astype(BF)
    here = 2 * y_half + y_part
    across = 2 * (1 - y_half) + (y_part ^ c)
    second_part, first_part = meet(y_second(part), y_first(part))
    last_part = y_first(second_part)
    weight_grad = place(jnp.stack([here, here ^ 1, across]).astype(jnp.int32), [part, second_part, first_part])
    weight_grad, last_part = meet(weight_grad, last_part)
    weight_grad = place((across ^ 1)[None].astype(jnp.int32), [last_part], weight_grad)
    return activated, input_grad, weight_grad


def solution(mesh):
    in_specs = (P(("fsdp", "rep"), None), P("fsdp", None), P(("fsdp", "rep"), None))
    out_specs = (P(("fsdp", "rep"), None), P(("fsdp", "rep"), None), P("fsdp", None))
    return jax.shard_map(local, mesh=mesh, in_specs=in_specs, out_specs=out_specs, check_vma=False)
```

```python
import functools
import math

import jax
import jax.numpy as jnp
from jax import lax
from jax.experimental import pallas as pl
from jax.experimental.pallas import tpu as pltpu
from jax.sharding import PartitionSpec as P

BF = jnp.bfloat16
F32 = jnp.float32
NX, NY = 4, 4
TILE = 512
ROWS = 384
PARTS = {"whole": 1, "halves": 2, "quarters": 4}
SMALL = pl.CostEstimate(flops=1, bytes_accessed=1, transcendentals=0)
COST = pl.CostEstimate(flops=10**13, bytes_accessed=10**10, transcendentals=0)
ROLES = ("own", "a", "b", "ab", "a_z", "b_z", "ab_z", "own_z")


def coords(f, r):
    return f // 4, r // 2, (f // 2) % 2, r % 2, f % 2


def permute(value, target):
    pairs = []
    for i in range(128):
        x, y, zh, zl, c = target(*coords(i // 8, i % 8))
        pairs.append((i, (x * 4 + zh * 2 + c) * 8 + y * 2 + zl))
    return lax.ppermute(value, ("fsdp", "rep"), pairs)


def first(i, c):
    return i ^ 1 if c == 0 else 3 - i


def second(i, c):
    return first(i, 1 - c)


def x_first(v):
    return permute(v, lambda x, y, zh, zl, c: (first(x, c), y, zh, zl, c))


def x_second(v):
    return permute(v, lambda x, y, zh, zl, c: (second(x, c), y, zh, zl, c))


def x_across(v):
    return permute(v, lambda x, y, zh, zl, c: ((x + 2) % 4, y, zh, zl, c))


def y_first(v):
    return permute(v, lambda x, y, zh, zl, c: (x, first(y, c), zh, zl, c))


def y_second(v):
    return permute(v, lambda x, y, zh, zl, c: (x, second(y, c), zh, zl, c))


def y_across(v):
    return permute(v, lambda x, y, zh, zl, c: (x, (y + 2) % 4, zh, zl, c))


def z_outer(v):
    return permute(v, lambda x, y, zh, zl, c: (x, y, 1 - zh, 1 - zl, c))


def z_inner(v):
    return permute(v, lambda x, y, zh, zl, c: (x, y, zh, 1 - zl, c))


def z_across(v):
    return permute(v, lambda x, y, zh, zl, c: (x, y, 1 - zh, zl, c))


def other_core(v):
    return permute(v, lambda x, y, zh, zl, c: (x, y, zh, zl, 1 - c))


def gelu_and_slope(pre, cot):
    k = math.sqrt(2.0 / math.pi)
    square = pre * pre
    t = jnp.tanh(pre * (k + (k * 0.044715) * square))
    half = 0.5 + 0.5 * t
    act = pre * half
    slope = half + (act - act * t) * (k + (3 * k * 0.044715) * square)
    return act.astype(BF), (cot.astype(F32) * slope).astype(BF)


def block_kernel(first, n_blocks, kind, scale, n_alias, folds, adds, at, tok_o, tok_p, *refs):
    n_sums = len(folds)
    w_in, refs = refs[:n_blocks], refs[n_blocks:]
    (cot_o, cot_p), refs = refs[:2], refs[2:]
    add_in, refs = refs[:adds], refs[adds:]
    earlier, refs = refs[: 2 * n_sums], refs[2 * n_sums + n_alias :]
    (act_o, act_p, slope_o, w_o), refs = refs[:4], refs[4:]
    part_o, refs = refs[: PARTS[kind]], refs[PARTS[kind] :]
    quarter_o, refs = refs[: n_sums > 0], refs[n_sums > 0 :]
    (tok, cot, w, act, slope, halves, load_sem, store_sem), refs = refs[:8], refs[8:]
    add, refs = refs[:adds], refs[adds:]
    m, rows, width = tok.shape[1], w.shape[1], halves.shape[3]
    loads, stores = [], []

    def load(src, dst):
        copy = pltpu.make_async_copy(src, dst, load_sem.at[len(loads)])
        copy.start()
        loads.append(copy)
        return copy

    def store(src, dst):
        copy = pltpu.make_async_copy(src, dst, store_sem.at[len(stores)])
        copy.start()
        stores.append(copy)

    def cols(k, width):
        return pl.ds(pl.multiple_of(k * width, width), width)

    y_half, y_part, y_other = at[first, 1], at[first, 2], at[first, 3]
    tok_loads, w_loads, cot_loads = [], [], []
    for k in range(n_blocks):
        w_loads.append(load(w_in[k], w.at[k]))
        for j in range(2):
            if k == 0:
                tok_in = (tok_o, tok_p)[j]
                tok_loads.append([load(tok_in.at[s : s + TILE], tok.at[j, s : s + TILE]) for s in range(0, m, TILE)])
            cot_loads.append(load((cot_o, cot_p)[j].at[:, cols(at[first + k, 0], rows)], cot.at[k, j]))
    order = (1 - y_half, y_half)
    add_loads = [load(add_in[0].at[:, cols(h, width)], add[0].at[k]) for k, h in enumerate(order * adds)]
    q = width // 2
    q_loads = []
    for k in range(n_sums):
        rows_at = pl.ds(sum(folds[:k]), folds[k])
        for h in range(2):
            q_loads.append(load(earlier[2 * k + h].at[:, cols(1 - y_part, q)], refs[0].at[h, rows_at]))

    for k in range(n_blocks):
        role = first + k
        w_loads[k].wait()
        place = slice(role * rows, (role + 1) * rows)
        act_out = (act_o.at[:, cols(at[role, 0], rows)], act_p.at[:, place])
        store(w.at[k], w_o.at[place])
        for j in range(2):
            cot_loads[2 * k + j].wait()
            for t, s in enumerate(range(0, m, TILE)):
                if k == 0:
                    tok_loads[j][t].wait()
                r = slice(s, s + TILE)
                pre = lax.dot_general(tok[j, r], w[k], (((1,), (1,)), ((), ())), preferred_element_type=F32)
                act[k, j, r], slope[k, j * m + s : j * m + s + TILE] = gelu_and_slope(pre, cot[k, j, r])
            store(act.at[k, j], act_out[j])
            mine = slice(j * m, (j + 1) * m)
            store(slope.at[k, mine], slope_o.at[mine, place])
        if k == 0 and n_sums:
            for copy in q_loads:
                copy.wait()
            refs[1][...] = (refs[0][0].astype(F32) + refs[0][1].astype(F32)).astype(BF)
            store(refs[1], quarter_o[0])
        for copy in add_loads if k == 0 else ():
            copy.wait()
        for h, half in enumerate(order):
            mine = cols(half, width)
            both = jnp.concatenate([tok[0, :, mine], tok[1, :, mine]], axis=0)
            term = lax.dot_general(slope[k], both, (((0,), (0,)), ((), ())), preferred_element_type=F32) * scale
            if adds:
                term += add[0][h].astype(F32)
            halves[k, h] = term.astype(BF)
            mine_rows = slice(k * rows, (k + 1) * rows)
            out = [v.at[mine_rows] for v in part_o]
            if kind == "whole":
                store(halves.at[k, h], out[0].at[:, mine])
            elif kind == "halves":
                store(halves.at[k, h], out[h])
            else:
                part = y_part if h else y_other
                store(halves.at[k, h, :, cols(part, q)], out[0 if h else 2])
                store(halves.at[k, h, :, cols(1 - part, q)], out[1 if h else 3])
    for copy in stores:
        copy.wait()


def block(first, at, tok_o, tok_p, w, kind, cot_o, cot_p, add, earlier, bufs, scale):
    m, d = tok_o.shape
    rows = w[0].shape[0]
    nb = len(w)
    n_all = cot_o.shape[1]
    folds = [pair[0].shape[0] for pair in earlier]
    quarter = (sum(folds), d // 4)
    shapes = [(m, n_all), (m, n_all // 2), (2 * m, n_all // 2), (n_all // 2, d)]
    shapes += [(nb * rows, d // PARTS[kind])] * PARTS[kind]
    shapes += [quarter] * (len(folds) > 0)
    args = [tok_o, tok_p, *w, cot_o, cot_p, *add, *[v for pair in earlier for v in pair], *bufs]
    adds = len(add)
    n_stores = 5 * nb + nb * max(2, PARTS[kind]) + 1
    out = pl.pallas_call(
        functools.partial(block_kernel, first, nb, kind, scale, len(bufs), folds, adds),
        grid_spec=pltpu.PrefetchScalarGridSpec(
            num_scalar_prefetch=1,
            grid=(1,),
            in_specs=[pl.BlockSpec(memory_space=pl.ANY)] * len(args),
            out_specs=[pl.BlockSpec(memory_space=pl.ANY)] * len(shapes),
            scratch_shapes=[
                pltpu.VMEM((2, m, d), BF),
                pltpu.VMEM((nb, 2, m, rows), BF),
                pltpu.VMEM((nb, rows, d), BF),
                pltpu.VMEM((nb, 2, m, rows), BF),
                pltpu.VMEM((nb, 2 * m, rows), BF),
                pltpu.VMEM((nb, 2, rows, d // 2), BF),
                pltpu.SemaphoreType.DMA((3 * nb + 2 * (m // TILE) + 2 * adds + 2 * len(folds),)),
                pltpu.SemaphoreType.DMA((n_stores,)),
            ]
            + [pltpu.VMEM((2, rows, d // 2), BF)] * adds
            + [pltpu.VMEM((2, *quarter), BF), pltpu.VMEM(quarter, BF)] * (len(folds) > 0),
        ),
        out_shape=[jax.ShapeDtypeStruct(s, BF) for s in shapes],
        input_output_aliases={1 + len(args) - len(bufs) + j: j for j in range(len(bufs))},
        compiler_params=pltpu.CompilerParams(vmem_limit_bytes=56 * 1024 * 1024),
        cost_estimate=COST,
        name=f"block_{first}",
    )(at, *args)
    return out[:4], *out[4:]


def place_kernel(n_parts, at, *refs):
    parts, out, (held, sems) = refs[:n_parts], refs[-3], refs[-2:]
    n = parts[0].shape[1]
    copies = []
    for j, part in enumerate(parts):
        held[j] = part[...].astype(F32)
        target = out.at[:, pl.ds(pl.multiple_of(at[j] * n, n), n)]
        copies.append(pltpu.make_async_copy(held.at[j], target, sems.at[j]))
        copies[-1].start()
    for copy in copies:
        copy.wait()


def place(at, parts, base=None):
    rows, n = parts[0].shape
    anywhere = pl.BlockSpec(memory_space=pl.ANY)
    some = base is not None
    return pl.pallas_call(
        functools.partial(place_kernel, len(parts)),
        grid_spec=pltpu.PrefetchScalarGridSpec(
            num_scalar_prefetch=1,
            grid=(1,),
            in_specs=[pl.BlockSpec((rows, n), lambda i, at: (0, 0))] * len(parts) + [anywhere] * some,
            out_specs=anywhere,
            scratch_shapes=[pltpu.VMEM((len(parts), rows, n), F32), pltpu.SemaphoreType.DMA((len(parts),))],
        ),
        out_shape=jax.ShapeDtypeStruct((rows, 4 * n), F32),
        input_output_aliases={1 + len(parts): 0} if some else {},
        compiler_params=pltpu.CompilerParams(vmem_limit_bytes=56 * 1024 * 1024),
        cost_estimate=COST,
        name="place",
    )(at, *parts, *([base] * some))


def grad_kernel(n_parts, *refs):
    slopes, ws, terms = refs[:n_parts], refs[n_parts : 2 * n_parts], refs[2 * n_parts : -1]
    total = jnp.dot(slopes[0][...], ws[0][...], preferred_element_type=F32)
    for slope, w in zip(slopes[1:], ws[1:]):
        total += jnp.dot(slope[...], w[...], preferred_element_type=F32)
    for term in terms:
        total += term[...]
    refs[-1][...] = total


def token_grad(part, slope, w, terms=(), depth=None, parts=(0,)):
    m, n = slope.shape[0] // 2, slope.shape[1]
    d = w.shape[1]
    depth = depth or n
    cols = 512
    tile = pl.BlockSpec((m, cols), lambda i: (0, i))
    return pl.pallas_call(
        functools.partial(grad_kernel, len(parts)),
        grid=(d // cols,),
        in_specs=[
            *[pl.BlockSpec((m, depth), lambda i, k=k: (part, k)) for k in parts],
            *[pl.BlockSpec((depth, cols), lambda i, k=k: (k, i)) for k in parts],
            *([tile] * len(terms)),
        ],
        out_specs=tile,
        out_shape=jax.ShapeDtypeStruct((m, d), F32),
        compiler_params=pltpu.CompilerParams(vmem_limit_bytes=56 * 1024 * 1024),
        cost_estimate=SMALL,
        name=f"token_grad_{part}",
    )(*[slope] * len(parts), *[w] * len(parts), *terms)


def finish_kernel(at, mine, other, *refs):
    i = pl.program_id(0)
    parts, _, out, act, held, sems = refs
    rows = held.shape[2]
    count = held.shape[0]

    def read(k):
        part = parts.at[:, k * rows : (k + 1) * rows]
        return pltpu.make_async_copy(part, held.at[k], sems.at[0, k])

    def write(k):
        target = act.at[:, pl.ds(pl.multiple_of(at[k] * rows, rows), rows)]
        return pltpu.make_async_copy(held.at[k], target, sems.at[1, k])

    @pl.when(i == 0)
    def _():
        for k in range(count):
            read(k).start()

    out[...] = mine[...] + other[...]

    @pl.when(i == 1)
    def _():
        for k in range(count):
            read(k).wait()
            write(k).start()

    @pl.when(i == pl.num_programs(0) - 1)
    def _():
        for k in range(count):
            write(k).wait()


def finish(at, mine, other, act, parts):
    m, d = mine.shape
    rows = ROWS
    tile = pl.BlockSpec((m // 4, d), lambda i, at: (i, 0))
    anywhere = pl.BlockSpec(memory_space=pl.ANY)
    count = parts.shape[1] // rows
    return pl.pallas_call(
        finish_kernel,
        grid_spec=pltpu.PrefetchScalarGridSpec(
            num_scalar_prefetch=1,
            grid=(4,),
            in_specs=[tile, tile] + [anywhere] * 2,
            out_specs=[tile, anywhere],
            scratch_shapes=[pltpu.VMEM((count, m, rows), BF), pltpu.SemaphoreType.DMA((2, count))],
        ),
        out_shape=[jax.ShapeDtypeStruct((m, d), F32), jax.ShapeDtypeStruct(act.shape, BF)],
        input_output_aliases={4: 1},
        compiler_params=pltpu.CompilerParams(vmem_limit_bytes=56 * 1024 * 1024),
        cost_estimate=SMALL,
        name="finish",
    )(at, mine, other, parts, act)


def local(tokens, weight, cotangent):
    m = tokens.shape[0]
    f, r = lax.axis_index("fsdp"), lax.axis_index("rep")
    x, y, zh, zl, c = coords(f, r)
    total_tokens = m * lax.axis_size("fsdp") * lax.axis_size("rep")
    scale = 1.0 / math.sqrt(total_tokens)

    y0, y1 = y % 2, y // 2
    y_half = jnp.where(c == 0, y0 ^ y1, y1)
    y_part = jnp.where(c == 0, y1, y0)

    def columns(c):
        xa = jnp.where(c == 0, x ^ 1, 3 - x)
        xb = jnp.where(c == 0, 3 - x, x ^ 1)
        at_x = {"own": x, "a": xa, "b": xb, "ab": (x + 2) % 4}
        return [
            4 * at_x[name.removesuffix("_z")] + 2 * (1 - zh if name.endswith("_z") else zh) + c for name in ROLES
        ]

    at = jnp.stack([v for col in columns(c) for v in (col, y_half, y_part, y_part ^ c)]).astype(jnp.int32).reshape(len(ROLES), -1)
    at_other = jnp.stack(columns(1 - c)).astype(jnp.int32)
    at_part = jnp.stack([y_part, 1 - y_part]).astype(jnp.int32)

    bufs = ()
    keep, got, got_q = {}, {}, {}

    def meet(*values):
        nonlocal at
        at, *values = lax.optimization_barrier((at, *values))
        return values

    def run(name, *w, fold=(), add=(), kind="halves"):
        nonlocal bufs
        first = ROLES.index(name)
        pairs = [(keep[k], got[k]) for k in fold]
        bufs, *out = block(first, at, tokens, tok_p, w, kind, cotangent, cot_p, add, pairs, bufs, scale)
        return out

    def quarter_to_send(name, row=0):
        return [(keep[name], row, 1), (got[name], row, 1)]

    def total(name, *others, row=0):
        return [(keep[name], row, 0), (got[name], row, 0), got_q[name], *others]

    def only(total, *more):
        def one(terms):
            value = 0.0
            for v, row, col in terms:
                v = v[row * ROWS : (row + 1) * ROWS]
                if col is not None:
                    v = lax.dynamic_slice_in_dim(v, at_part[col] * (v.shape[1] // 2), v.shape[1] // 2, 1)
                value += v.astype(F32)
            return value.astype(BF)

        return jnp.concatenate([one(terms) for terms in (total, *more)]) if more else one(total)

    tok_p = other_core(tokens)
    cot_p = other_core(cotangent)
    own = weight.astype(BF)
    a = x_first(own)
    oz = z_outer(own)

    tok_p, cot_p, own = meet(tok_p, cot_p, own)
    b = x_second(own)
    send, keep["own"] = run("own", own)

    send, a = meet(send, a)
    got["own"], az = y_first(send), z_outer(a)
    send, keep["a"] = run("a", a)

    send, b, got["own"] = meet(send, b, got["own"])
    got["a"], ab = y_first(send), x_first(b)
    send, keep["b"] = run("b", b)

    send, slope, w_all = meet(send, *bufs[2:])
    bufs = [*bufs[:2], slope, w_all]
    grad_o = token_grad(0, slope, w_all, depth=2 * ROWS)
    send, grad_o, ab, got["a"], oz = meet(send, grad_o, ab, got["a"], oz)
    got["b"], bz = y_first(send), x_second(oz)
    send, keep["ab"], q = run("ab", ab, fold=("own", "a"))

    send, q, got["b"], az = meet(send, q, got["b"], az)
    got["ab"], got_two, abz = y_first(send), y_second(q), x_second(az)
    (whole,) = run("a_z", az, kind="whole")

    whole, got["ab"], got_two, bz = meet(whole, got["ab"], got_two, bz)
    got_q["own"], got_q["a"] = (got_two, 0, None), (got_two, 1, None)
    got_two = y_second(only(quarter_to_send("b"), quarter_to_send("ab")))
    whole, abz = meet(whole, abz)
    whole = x_first(whole)
    parts = run("b_z", bz, abz, kind="quarters")

    *parts, got_two = meet(*parts, got_two)
    got_q["b"], got_q["ab"] = (got_two, 0, None), (got_two, 1, None)
    parts = [parts[0], y_second(parts[1]), y_first(parts[2]), y_across(parts[3])]
    got_x = x_second(only(total("b"), total("ab")))
    oz_parts = run("own_z", oz, add=(whole,), kind="quarters")
    act, act_p, slope, w_all = bufs

    *oz_parts, slope, got_x = meet(*oz_parts, slope, got_x)
    got_x1 = x_first(only(total("a", (got_x, 1, None))))
    grad_p = token_grad(1, slope, w_all)

    *parts, grad_p, got_x, got_x1 = meet(*parts, grad_p, got_x, got_x1)
    got_oz = [y_second(oz_parts[1]), y_first(oz_parts[2]), y_across(oz_parts[3])]
    got_x2, got_x3 = (
        permuted(only([(v, row, None) for v in parts])) for row, permuted in enumerate((x_second, x_across))
    )
    grad_o = token_grad(0, slope, w_all, (grad_o,), depth=2 * ROWS, parts=(1, 2, 3))

    got_x2, got_x3, *got_oz, grad_o, grad_p, act_p = meet(got_x2, got_x3, *got_oz, grad_o, grad_p, act_p)
    other = only([(v, 0, None) for v in (oz_parts[0], *got_oz, got_x2, got_x3)])
    z1, z2 = z_outer(other), z_across(other)
    swapped = other_core(grad_p)
    same = only(total("own", (got_x, 0, None), (got_x1, 0, None)))
    same_z = z_inner(same)
    act_p = other_core(act_p)
    input_grad, activated = finish(at_other, grad_o, swapped, act, act_p)

    z1, z2, same_z, input_grad = meet(z1, z2, same_z, input_grad)

    part = sum(v.astype(F32) for v in (same, same_z, z1, z2)).astype(BF)
    here = 2 * y_half + y_part
    across = 2 * (1 - y_half) + (y_part ^ c)
    second_part, first_part = meet(y_second(part), y_first(part))
    last_part = y_first(second_part)
    weight_grad = place(jnp.stack([here, here ^ 1, across]).astype(jnp.int32), [part, second_part, first_part])
    weight_grad, last_part = meet(weight_grad, last_part)
    weight_grad = place((across ^ 1)[None].astype(jnp.int32), [last_part], weight_grad)
    return activated, input_grad, weight_grad


def solution(mesh):
    in_specs = (P(("fsdp", "rep"), None), P("fsdp", None), P(("fsdp", "rep"), None))
    out_specs = (P(("fsdp", "rep"), None), P(("fsdp", "rep"), None), P("fsdp", None))
    return jax.shard_map(local, mesh=mesh, in_specs=in_specs, out_specs=out_specs, check_vma=False)
```

```python
import functools
import math

import jax
import jax.numpy as jnp
from jax import lax
from jax.experimental import pallas as pl
from jax.experimental.pallas import tpu as pltpu
from jax.sharding import PartitionSpec as P

BF = jnp.bfloat16
F32 = jnp.float32
NX, NY = 4, 4
TILE = 512
ROWS = 384
PARTS = {"whole": 1, "halves": 2, "quarters": 4}
SMALL = pl.CostEstimate(flops=1, bytes_accessed=1, transcendentals=0)
COST = pl.CostEstimate(flops=10**13, bytes_accessed=10**10, transcendentals=0)
ROLES = ("own", "a", "b", "ab", "a_z", "b_z", "ab_z", "own_z")


def coords(f, r):
    return f // 4, r // 2, (f // 2) % 2, r % 2, f % 2


def permute(value, target):
    pairs = []
    for i in range(128):
        x, y, zh, zl, c = target(*coords(i // 8, i % 8))
        pairs.append((i, (x * 4 + zh * 2 + c) * 8 + y * 2 + zl))
    return lax.ppermute(value, ("fsdp", "rep"), pairs)


def first(i, c):
    return i ^ 1 if c == 0 else 3 - i


def second(i, c):
    return first(i, 1 - c)


def x_first(v):
    return permute(v, lambda x, y, zh, zl, c: (first(x, c), y, zh, zl, c))


def x_second(v):
    return permute(v, lambda x, y, zh, zl, c: (second(x, c), y, zh, zl, c))


def x_across(v):
    return permute(v, lambda x, y, zh, zl, c: ((x + 2) % 4, y, zh, zl, c))


def y_first(v):
    return permute(v, lambda x, y, zh, zl, c: (x, first(y, c), zh, zl, c))


def y_second(v):
    return permute(v, lambda x, y, zh, zl, c: (x, second(y, c), zh, zl, c))


def y_across(v):
    return permute(v, lambda x, y, zh, zl, c: (x, (y + 2) % 4, zh, zl, c))


def z_outer(v):
    return permute(v, lambda x, y, zh, zl, c: (x, y, 1 - zh, 1 - zl, c))


def z_inner(v):
    return permute(v, lambda x, y, zh, zl, c: (x, y, zh, 1 - zl, c))


def z_across(v):
    return permute(v, lambda x, y, zh, zl, c: (x, y, 1 - zh, zl, c))


def other_core(v):
    return permute(v, lambda x, y, zh, zl, c: (x, y, zh, zl, 1 - c))


def gelu_and_slope(pre, cot):
    k = math.sqrt(2.0 / math.pi)
    square = pre * pre
    t = jnp.tanh(pre * (k + (k * 0.044715) * square))
    half = 0.5 + 0.5 * t
    act = pre * half
    slope = half + (act - act * t) * (k + (3 * k * 0.044715) * square)
    return act.astype(BF), (cot.astype(F32) * slope).astype(BF)


def block_kernel(first, n_blocks, kind, scale, n_alias, folds, adds, at, tok_o, tok_p, *refs):
    n_sums = len(folds)
    w_in, refs = refs[:n_blocks], refs[n_blocks:]
    (cot_o, cot_p), refs = refs[:2], refs[2:]
    add_in, refs = refs[:adds], refs[adds:]
    earlier, refs = refs[: 2 * n_sums], refs[2 * n_sums + n_alias :]
    (act_o, act_p, slope_o, w_o), refs = refs[:4], refs[4:]
    part_o, refs = refs[: PARTS[kind]], refs[PARTS[kind] :]
    quarter_o, refs = refs[: n_sums > 0], refs[n_sums > 0 :]
    (tok, cot, w, act, slope, halves, load_sem, store_sem), refs = refs[:8], refs[8:]
    add, refs = refs[:adds], refs[adds:]
    m, rows, width = tok.shape[1], w.shape[1], halves.shape[3]
    loads, stores = [], []

    def load(src, dst):
        copy = pltpu.make_async_copy(src, dst, load_sem.at[len(loads)])
        copy.start()
        loads.append(copy)
        return copy

    def store(src, dst):
        copy = pltpu.make_async_copy(src, dst, store_sem.at[len(stores)])
        copy.start()
        stores.append(copy)

    def cols(k, width):
        return pl.ds(pl.multiple_of(k * width, width), width)

    y_half, y_part, y_other = at[first, 1], at[first, 2], at[first, 3]
    tok_loads, w_loads, cot_loads = [], [], []
    for k in range(n_blocks):
        w_loads.append(load(w_in[k], w.at[k]))
        for j in range(2):
            if k == 0:
                tok_in = (tok_o, tok_p)[j]
                tok_loads.append([load(tok_in.at[s : s + TILE], tok.at[j, s : s + TILE]) for s in range(0, m, TILE)])
            cot_loads.append(load((cot_o, cot_p)[j].at[:, cols(at[first + k, 0], rows)], cot.at[k, j]))
    order = (1 - y_half, y_half)
    add_loads = [load(add_in[0].at[:, cols(h, width)], add[0].at[k]) for k, h in enumerate(order * adds)]
    q = width // 2
    q_loads = []
    for k in range(n_sums):
        rows_at = pl.ds(sum(folds[:k]), folds[k])
        for h in range(2):
            q_loads.append(load(earlier[2 * k + h].at[:, cols(1 - y_part, q)], refs[0].at[h, rows_at]))

    for k in range(n_blocks):
        role = first + k
        w_loads[k].wait()
        place = slice(role * rows, (role + 1) * rows)
        act_out = (act_o.at[:, cols(at[role, 0], rows)], act_p.at[:, place])
        store(w.at[k], w_o.at[place])
        for j in range(2):
            cot_loads[2 * k + j].wait()
            for t, s in enumerate(range(0, m, TILE)):
                if k == 0:
                    tok_loads[j][t].wait()
                r = slice(s, s + TILE)
                pre = lax.dot_general(tok[j, r], w[k], (((1,), (1,)), ((), ())), preferred_element_type=F32)
                act[k, j, r], slope[k, j * m + s : j * m + s + TILE] = gelu_and_slope(pre, cot[k, j, r])
            store(act.at[k, j], act_out[j])
            mine = slice(j * m, (j + 1) * m)
            store(slope.at[k, mine], slope_o.at[mine, place])
        if k == 0 and n_sums:
            for copy in q_loads:
                copy.wait()
            refs[1][...] = (refs[0][0].astype(F32) + refs[0][1].astype(F32)).astype(BF)
            store(refs[1], quarter_o[0])
        for copy in add_loads if k == 0 else ():
            copy.wait()
        for h, half in enumerate(order):
            mine = cols(half, width)
            both = jnp.concatenate([tok[0, :, mine], tok[1, :, mine]], axis=0)
            term = lax.dot_general(slope[k], both, (((0,), (0,)), ((), ())), preferred_element_type=F32) * scale
            if adds:
                term += add[0][h].astype(F32)
            halves[k, h] = term.astype(BF)
            mine_rows = slice(k * rows, (k + 1) * rows)
            out = [v.at[mine_rows] for v in part_o]
            if kind == "whole":
                store(halves.at[k, h], out[0].at[:, mine])
            elif kind == "halves":
                store(halves.at[k, h], out[h])
            else:
                part = y_part if h else y_other
                store(halves.at[k, h, :, cols(part, q)], out[0 if h else 2])
                store(halves.at[k, h, :, cols(1 - part, q)], out[1 if h else 3])
    for copy in stores:
        copy.wait()


def block(first, at, tok_o, tok_p, w, kind, cot_o, cot_p, add, earlier, bufs, scale):
    m, d = tok_o.shape
    rows = w[0].shape[0]
    nb = len(w)
    n_all = cot_o.shape[1]
    folds = [pair[0].shape[0] for pair in earlier]
    quarter = (sum(folds), d // 4)
    shapes = [(m, n_all), (m, n_all // 2), (2 * m, n_all // 2), (n_all // 2, d)]
    shapes += [(nb * rows, d // PARTS[kind])] * PARTS[kind]
    shapes += [quarter] * (len(folds) > 0)
    args = [tok_o, tok_p, *w, cot_o, cot_p, *add, *[v for pair in earlier for v in pair], *bufs]
    adds = len(add)
    n_stores = 5 * nb + nb * max(2, PARTS[kind]) + 1
    out = pl.pallas_call(
        functools.partial(block_kernel, first, nb, kind, scale, len(bufs), folds, adds),
        grid_spec=pltpu.PrefetchScalarGridSpec(
            num_scalar_prefetch=1,
            grid=(1,),
            in_specs=[pl.BlockSpec(memory_space=pl.ANY)] * len(args),
            out_specs=[pl.BlockSpec(memory_space=pl.ANY)] * len(shapes),
            scratch_shapes=[
                pltpu.VMEM((2, m, d), BF),
                pltpu.VMEM((nb, 2, m, rows), BF),
                pltpu.VMEM((nb, rows, d), BF),
                pltpu.VMEM((nb, 2, m, rows), BF),
                pltpu.VMEM((nb, 2 * m, rows), BF),
                pltpu.VMEM((nb, 2, rows, d // 2), BF),
                pltpu.SemaphoreType.DMA((3 * nb + 2 * (m // TILE) + 2 * adds + 2 * len(folds),)),
                pltpu.SemaphoreType.DMA((n_stores,)),
            ]
            + [pltpu.VMEM((2, rows, d // 2), BF)] * adds
            + [pltpu.VMEM((2, *quarter), BF), pltpu.VMEM(quarter, BF)] * (len(folds) > 0),
        ),
        out_shape=[jax.ShapeDtypeStruct(s, BF) for s in shapes],
        input_output_aliases={1 + len(args) - len(bufs) + j: j for j in range(len(bufs))},
        compiler_params=pltpu.CompilerParams(vmem_limit_bytes=56 * 1024 * 1024),
        cost_estimate=COST if 0 < first < 4 else SMALL,
        name=f"block_{first}",
    )(at, *args)
    return out[:4], *out[4:]


def place_kernel(n_parts, at, *refs):
    parts, out, (held, sems) = refs[:n_parts], refs[-3], refs[-2:]
    n = parts[0].shape[1]
    copies = []
    for j, part in enumerate(parts):
        held[j] = part[...].astype(F32)
        target = out.at[:, pl.ds(pl.multiple_of(at[j] * n, n), n)]
        copies.append(pltpu.make_async_copy(held.at[j], target, sems.at[j]))
        copies[-1].start()
    for copy in copies:
        copy.wait()


def place(at, parts, base=None):
    rows, n = parts[0].shape
    anywhere = pl.BlockSpec(memory_space=pl.ANY)
    some = base is not None
    return pl.pallas_call(
        functools.partial(place_kernel, len(parts)),
        grid_spec=pltpu.PrefetchScalarGridSpec(
            num_scalar_prefetch=1,
            grid=(1,),
            in_specs=[pl.BlockSpec((rows, n), lambda i, at: (0, 0))] * len(parts) + [anywhere] * some,
            out_specs=anywhere,
            scratch_shapes=[pltpu.VMEM((len(parts), rows, n), F32), pltpu.SemaphoreType.DMA((len(parts),))],
        ),
        out_shape=jax.ShapeDtypeStruct((rows, 4 * n), F32),
        input_output_aliases={1 + len(parts): 0} if some else {},
        compiler_params=pltpu.CompilerParams(vmem_limit_bytes=56 * 1024 * 1024),
        cost_estimate=COST,
        name="place",
    )(at, *parts, *([base] * some))


def grad_kernel(n_parts, *refs):
    slopes, ws, terms = refs[:n_parts], refs[n_parts : 2 * n_parts], refs[2 * n_parts : -1]
    total = jnp.dot(slopes[0][...], ws[0][...], preferred_element_type=F32)
    for slope, w in zip(slopes[1:], ws[1:]):
        total += jnp.dot(slope[...], w[...], preferred_element_type=F32)
    for term in terms:
        total += term[...]
    refs[-1][...] = total.astype(refs[-1].dtype)


def token_grad(part, slope, w, terms=(), depth=None, parts=(0,), kind=F32):
    m, n = slope.shape[0] // 2, slope.shape[1]
    d = w.shape[1]
    depth = depth or n
    cols = 512
    tile = pl.BlockSpec((m, cols), lambda i: (0, i))
    return pl.pallas_call(
        functools.partial(grad_kernel, len(parts)),
        grid=(d // cols,),
        in_specs=[
            *[pl.BlockSpec((m, depth), lambda i, k=k: (part, k)) for k in parts],
            *[pl.BlockSpec((depth, cols), lambda i, k=k: (k, i)) for k in parts],
            *([tile] * len(terms)),
        ],
        out_specs=tile,
        out_shape=jax.ShapeDtypeStruct((m, d), kind),
        compiler_params=pltpu.CompilerParams(vmem_limit_bytes=56 * 1024 * 1024),
        cost_estimate=SMALL,
        name=f"token_grad_{part}",
    )(*[slope] * len(parts), *[w] * len(parts), *terms)


def finish_kernel(at, mine, other, *refs):
    i = pl.program_id(0)
    parts, _, out, act, held, sems = refs
    rows = held.shape[2]
    count = held.shape[0]

    def read(k):
        part = parts.at[:, k * rows : (k + 1) * rows]
        return pltpu.make_async_copy(part, held.at[k], sems.at[0, k])

    def write(k):
        target = act.at[:, pl.ds(pl.multiple_of(at[k] * rows, rows), rows)]
        return pltpu.make_async_copy(held.at[k], target, sems.at[1, k])

    @pl.when(i == 0)
    def _():
        for k in range(count):
            read(k).start()

    out[...] = mine[...] + other[...].astype(F32)

    @pl.when(i == 1)
    def _():
        for k in range(count):
            read(k).wait()
            write(k).start()

    @pl.when(i == pl.num_programs(0) - 1)
    def _():
        for k in range(count):
            write(k).wait()


def finish(at, mine, other, act, parts):
    m, d = mine.shape
    rows = ROWS
    tile = pl.BlockSpec((m // 4, d), lambda i, at: (i, 0))
    anywhere = pl.BlockSpec(memory_space=pl.ANY)
    count = parts.shape[1] // rows
    return pl.pallas_call(
        finish_kernel,
        grid_spec=pltpu.PrefetchScalarGridSpec(
            num_scalar_prefetch=1,
            grid=(4,),
            in_specs=[tile, tile] + [anywhere] * 2,
            out_specs=[tile, anywhere],
            scratch_shapes=[pltpu.VMEM((count, m, rows), BF), pltpu.SemaphoreType.DMA((2, count))],
        ),
        out_shape=[jax.ShapeDtypeStruct((m, d), F32), jax.ShapeDtypeStruct(act.shape, BF)],
        input_output_aliases={4: 1},
        compiler_params=pltpu.CompilerParams(vmem_limit_bytes=56 * 1024 * 1024),
        cost_estimate=SMALL,
        name="finish",
    )(at, mine, other, parts, act)


def local(tokens, weight, cotangent):
    m = tokens.shape[0]
    f, r = lax.axis_index("fsdp"), lax.axis_index("rep")
    x, y, zh, zl, c = coords(f, r)
    total_tokens = m * lax.axis_size("fsdp") * lax.axis_size("rep")
    scale = 1.0 / math.sqrt(total_tokens)

    y0, y1 = y % 2, y // 2
    y_half = jnp.where(c == 0, y0 ^ y1, y1)
    y_part = jnp.where(c == 0, y1, y0)

    def columns(c):
        xa = jnp.where(c == 0, x ^ 1, 3 - x)
        xb = jnp.where(c == 0, 3 - x, x ^ 1)
        at_x = {"own": x, "a": xa, "b": xb, "ab": (x + 2) % 4}
        return [
            4 * at_x[name.removesuffix("_z")] + 2 * (1 - zh if name.endswith("_z") else zh) + c for name in ROLES
        ]

    at = jnp.stack([v for col in columns(c) for v in (col, y_half, y_part, y_part ^ c)]).astype(jnp.int32).reshape(len(ROLES), -1)
    at_other = jnp.stack(columns(1 - c)).astype(jnp.int32)
    at_part = jnp.stack([y_part, 1 - y_part]).astype(jnp.int32)

    bufs = ()
    keep, got, got_q = {}, {}, {}

    def meet(*values):
        nonlocal at
        at, *values = lax.optimization_barrier((at, *values))
        return values

    def run(name, *w, fold=(), add=(), kind="halves"):
        nonlocal bufs
        first = ROLES.index(name)
        pairs = [(keep[k], got[k]) for k in fold]
        bufs, *out = block(first, at, tokens, tok_p, w, kind, cotangent, cot_p, add, pairs, bufs, scale)
        return out

    def quarter_to_send(name, row=0):
        return [(keep[name], row, 1), (got[name], row, 1)]

    def total(name, *others, row=0):
        return [(keep[name], row, 0), (got[name], row, 0), got_q[name], *others]

    def only(total, *more):
        def one(terms):
            value = 0.0
            for v, row, col in terms:
                v = v[row * ROWS : (row + 1) * ROWS]
                if col is not None:
                    v = lax.dynamic_slice_in_dim(v, at_part[col] * (v.shape[1] // 2), v.shape[1] // 2, 1)
                value += v.astype(F32)
            return value.astype(BF)

        return jnp.concatenate([one(terms) for terms in (total, *more)]) if more else one(total)

    tok_p = other_core(tokens)
    cot_p = other_core(cotangent)
    own = weight.astype(BF)
    a = x_first(own)
    oz = z_outer(own)

    tok_p, cot_p, own = meet(tok_p, cot_p, own)
    b = x_second(own)
    send, keep["own"] = run("own", own)

    send, a = meet(send, a)
    got["own"], az = y_first(send), z_outer(a)
    send, keep["a"] = run("a", a)

    send, b, got["own"] = meet(send, b, got["own"])
    got["a"], ab = y_first(send), x_first(b)
    send, keep["b"] = run("b", b)

    send, slope, w_all = meet(send, *bufs[2:])
    bufs = [*bufs[:2], slope, w_all]
    grad_o = token_grad(0, slope, w_all, depth=2 * ROWS)
    send, grad_o, ab, got["a"], oz = meet(send, grad_o, ab, got["a"], oz)
    got["b"], bz = y_first(send), x_second(oz)
    send, keep["ab"], q = run("ab", ab, fold=("own", "a"))

    send, q, got["b"], az = meet(send, q, got["b"], az)
    got["ab"], got_two, abz = y_first(send), y_second(q), x_second(az)
    (whole,) = run("a_z", az, kind="whole")

    whole, got["ab"], got_two, bz = meet(whole, got["ab"], got_two, bz)
    got_q["own"], got_q["a"] = (got_two, 0, None), (got_two, 1, None)
    got_two = y_second(only(quarter_to_send("b"), quarter_to_send("ab")))
    whole, abz = meet(whole, abz)
    whole = x_first(whole)
    parts = run("b_z", bz, abz, kind="quarters")

    *parts, got_two = meet(*parts, got_two)
    got_q["b"], got_q["ab"] = (got_two, 0, None), (got_two, 1, None)
    parts = [parts[0], y_second(parts[1]), y_first(parts[2]), y_across(parts[3])]
    got_x = x_second(only(total("b"), total("ab")))
    oz_parts = run("own_z", oz, add=(whole,), kind="quarters")
    act, act_p, slope, w_all = bufs

    *oz_parts, slope, got_x = meet(*oz_parts, slope, got_x)
    got_x1 = x_first(only(total("a", (got_x, 1, None))))
    grad_p = token_grad(1, slope, w_all, kind=BF)

    *parts, grad_p, got_x, got_x1 = meet(*parts, grad_p, got_x, got_x1)
    got_oz = [y_second(oz_parts[1]), y_first(oz_parts[2]), y_across(oz_parts[3])]
    got_x2, got_x3 = (
        permuted(only([(v, row, None) for v in parts])) for row, permuted in enumerate((x_second, x_across))
    )
    same = only(total("own", (got_x, 0, None), (got_x1, 0, None)))
    grad_o = token_grad(0, slope, w_all, (grad_o,), depth=2 * ROWS, parts=(1, 2, 3))

    got_x2, got_x3, *got_oz, grad_o, same = meet(got_x2, got_x3, *got_oz, grad_o, same)
    other = only([(v, 0, None) for v in (oz_parts[0], *got_oz, got_x2, got_x3)])
    other, same, grad_p, act_p = meet(other, same, grad_p, act_p)
    z1, z2, same_z = z_outer(other), z_across(other), z_inner(same)
    swapped, act_p = other_core(grad_p), other_core(act_p)
    input_grad, activated = finish(at_other, grad_o, swapped, act, act_p)

    z1, z2, same_z, input_grad = meet(z1, z2, same_z, input_grad)

    part = sum(v.astype(F32) for v in (same, same_z, z1, z2)).astype(BF)
    here = 2 * y_half + y_part
    across = 2 * (1 - y_half) + (y_part ^ c)
    second_part, first_part = meet(y_second(part), y_first(part))
    last_part = y_first(second_part)
    weight_grad = place(jnp.stack([here, here ^ 1, across]).astype(jnp.int32), [part, second_part, first_part])
    weight_grad, last_part = meet(weight_grad, last_part)
    weight_grad = place((across ^ 1)[None].astype(jnp.int32), [last_part], weight_grad)
    return activated, input_grad, weight_grad


def solution(mesh):
    in_specs = (P(("fsdp", "rep"), None), P("fsdp", None), P(("fsdp", "rep"), None))
    out_specs = (P(("fsdp", "rep"), None), P(("fsdp", "rep"), None), P("fsdp", None))
    return jax.shard_map(local, mesh=mesh, in_specs=in_specs, out_specs=out_specs, check_vma=False)
```

```python
import functools
import math

import jax
import jax.numpy as jnp
from jax import lax
from jax.experimental import pallas as pl
from jax.experimental.pallas import tpu as pltpu
from jax.sharding import PartitionSpec as P

BF = jnp.bfloat16
F32 = jnp.float32
NX, NY = 4, 4
TILE = 512
ROWS = 384
PARTS = {"whole": 1, "halves": 2, "quarters": 4}
SMALL = pl.CostEstimate(flops=1, bytes_accessed=1, transcendentals=0)
COST = pl.CostEstimate(flops=10**13, bytes_accessed=10**10, transcendentals=0)
ROLES = ("own", "a", "b", "ab", "a_z", "b_z", "ab_z", "own_z")


def coords(f, r):
    return f // 4, r // 2, (f // 2) % 2, r % 2, f % 2


def permute(value, target):
    pairs = []
    for i in range(128):
        x, y, zh, zl, c = target(*coords(i // 8, i % 8))
        pairs.append((i, (x * 4 + zh * 2 + c) * 8 + y * 2 + zl))
    return lax.ppermute(value, ("fsdp", "rep"), pairs)


def first(i, c):
    return i ^ 1 if c == 0 else 3 - i


def second(i, c):
    return first(i, 1 - c)


def x_first(v):
    return permute(v, lambda x, y, zh, zl, c: (first(x, c), y, zh, zl, c))


def x_second(v):
    return permute(v, lambda x, y, zh, zl, c: (second(x, c), y, zh, zl, c))


def x_across(v):
    return permute(v, lambda x, y, zh, zl, c: ((x + 2) % 4, y, zh, zl, c))


def y_first(v):
    return permute(v, lambda x, y, zh, zl, c: (x, first(y, c), zh, zl, c))


def y_second(v):
    return permute(v, lambda x, y, zh, zl, c: (x, second(y, c), zh, zl, c))


def y_across(v):
    return permute(v, lambda x, y, zh, zl, c: (x, (y + 2) % 4, zh, zl, c))


def z_outer(v):
    return permute(v, lambda x, y, zh, zl, c: (x, y, 1 - zh, 1 - zl, c))


def z_inner(v):
    return permute(v, lambda x, y, zh, zl, c: (x, y, zh, 1 - zl, c))


def z_across(v):
    return permute(v, lambda x, y, zh, zl, c: (x, y, 1 - zh, zl, c))


def other_core(v):
    return permute(v, lambda x, y, zh, zl, c: (x, y, zh, zl, 1 - c))


def gelu_and_slope(pre, cot):
    k = math.sqrt(2.0 / math.pi)
    square = pre * pre
    t = jnp.tanh(pre * (k + (k * 0.044715) * square))
    half = 0.5 + 0.5 * t
    act = pre * half
    slope = half + (act - act * t) * (k + (3 * k * 0.044715) * square)
    return act.astype(BF), (cot.astype(F32) * slope).astype(BF)


def block_kernel(first, n_blocks, kind, scale, n_alias, folds, adds, at, tok_o, tok_p, *refs):
    n_sums = len(folds)
    w_in, refs = refs[:n_blocks], refs[n_blocks:]
    (cot_o, cot_p), refs = refs[:2], refs[2:]
    add_in, refs = refs[:adds], refs[adds:]
    earlier, refs = refs[: 2 * n_sums], refs[2 * n_sums + n_alias :]
    (act_o, act_p, slope_o, w_o), refs = refs[:4], refs[4:]
    part_o, refs = refs[: PARTS[kind]], refs[PARTS[kind] :]
    quarter_o, refs = refs[: n_sums > 0], refs[n_sums > 0 :]
    (tok, cot, w, act, slope, halves, load_sem, store_sem), refs = refs[:8], refs[8:]
    add, refs = refs[:adds], refs[adds:]
    m, rows, width = tok.shape[1], w.shape[1], halves.shape[3]
    loads, stores = [], []

    def load(src, dst):
        copy = pltpu.make_async_copy(src, dst, load_sem.at[len(loads)])
        copy.start()
        loads.append(copy)
        return copy

    def store(src, dst):
        copy = pltpu.make_async_copy(src, dst, store_sem.at[len(stores)])
        copy.start()
        stores.append(copy)

    def cols(k, width):
        return pl.ds(pl.multiple_of(k * width, width), width)

    y_half, y_part, y_other = at[first, 1], at[first, 2], at[first, 3]
    tok_loads, w_loads, cot_loads = [], [], []
    for k in range(n_blocks):
        w_loads.append(load(w_in[k], w.at[k]))
        for j in range(2):
            if k == 0:
                tok_in = (tok_o, tok_p)[j]
                tok_loads.append([load(tok_in.at[s : s + TILE], tok.at[j, s : s + TILE]) for s in range(0, m, TILE)])
            cot_loads.append(load((cot_o, cot_p)[j].at[:, cols(at[first + k, 0], rows)], cot.at[k, j]))
    order = (1 - y_half, y_half)
    add_loads = [load(add_in[0].at[:, cols(h, width)], add[0].at[k]) for k, h in enumerate(order * adds)]
    q = width // 2
    q_loads = []
    for k in range(n_sums):
        rows_at = pl.ds(sum(folds[:k]), folds[k])
        for h in range(2):
            q_loads.append(load(earlier[2 * k + h].at[:, cols(1 - y_part, q)], refs[0].at[h, rows_at]))

    for k in range(n_blocks):
        role = first + k
        w_loads[k].wait()
        place = slice(role * rows, (role + 1) * rows)
        act_out = (act_o.at[:, cols(at[role, 0], rows)], act_p.at[:, place])
        store(w.at[k], w_o.at[place])
        for j in range(2):
            cot_loads[2 * k + j].wait()
            for t, s in enumerate(range(0, m, TILE)):
                if k == 0:
                    tok_loads[j][t].wait()
                r = slice(s, s + TILE)
                pre = lax.dot_general(tok[j, r], w[k], (((1,), (1,)), ((), ())), preferred_element_type=F32)
                act[k, j, r], slope[k, j * m + s : j * m + s + TILE] = gelu_and_slope(pre, cot[k, j, r])
            store(act.at[k, j], act_out[j])
            mine = slice(j * m, (j + 1) * m)
            store(slope.at[k, mine], slope_o.at[mine, place])
        if k == 0 and n_sums:
            for copy in q_loads:
                copy.wait()
            refs[1][...] = (refs[0][0].astype(F32) + refs[0][1].astype(F32)).astype(BF)
            store(refs[1], quarter_o[0])
        for copy in add_loads if k == 0 else ():
            copy.wait()
        for h, half in enumerate(order):
            mine = cols(half, width)
            both = jnp.concatenate([tok[0, :, mine], tok[1, :, mine]], axis=0)
            term = lax.dot_general(slope[k], both, (((0,), (0,)), ((), ())), preferred_element_type=F32) * scale
            if adds:
                term += add[0][h].astype(F32)
            halves[k, h] = term.astype(BF)
            mine_rows = slice(k * rows, (k + 1) * rows)
            out = [v.at[mine_rows] for v in part_o]
            if kind == "whole":
                store(halves.at[k, h], out[0].at[:, mine])
            elif kind == "halves":
                store(halves.at[k, h], out[h])
            else:
                part = y_part if h else y_other
                store(halves.at[k, h, :, cols(part, q)], out[0 if h else 2])
                store(halves.at[k, h, :, cols(1 - part, q)], out[1 if h else 3])
    for copy in stores:
        copy.wait()


def block(first, at, tok_o, tok_p, w, kind, cot_o, cot_p, add, earlier, bufs, scale):
    m, d = tok_o.shape
    rows = w[0].shape[0]
    nb = len(w)
    n_all = cot_o.shape[1]
    folds = [pair[0].shape[0] for pair in earlier]
    quarter = (sum(folds), d // 4)
    shapes = [(m, n_all), (m, n_all // 2), (2 * m, n_all // 2), (n_all // 2, d)]
    shapes += [(nb * rows, d // PARTS[kind])] * PARTS[kind]
    shapes += [quarter] * (len(folds) > 0)
    args = [tok_o, tok_p, *w, cot_o, cot_p, *add, *[v for pair in earlier for v in pair], *bufs]
    adds = len(add)
    n_stores = 5 * nb + nb * max(2, PARTS[kind]) + 1
    out = pl.pallas_call(
        functools.partial(block_kernel, first, nb, kind, scale, len(bufs), folds, adds),
        grid_spec=pltpu.PrefetchScalarGridSpec(
            num_scalar_prefetch=1,
            grid=(1,),
            in_specs=[pl.BlockSpec(memory_space=pl.ANY)] * len(args),
            out_specs=[pl.BlockSpec(memory_space=pl.ANY)] * len(shapes),
            scratch_shapes=[
                pltpu.VMEM((2, m, d), BF),
                pltpu.VMEM((nb, 2, m, rows), BF),
                pltpu.VMEM((nb, rows, d), BF),
                pltpu.VMEM((nb, 2, m, rows), BF),
                pltpu.VMEM((nb, 2 * m, rows), BF),
                pltpu.VMEM((nb, 2, rows, d // 2), BF),
                pltpu.SemaphoreType.DMA((3 * nb + 2 * (m // TILE) + 2 * adds + 2 * len(folds),)),
                pltpu.SemaphoreType.DMA((n_stores,)),
            ]
            + [pltpu.VMEM((2, rows, d // 2), BF)] * adds
            + [pltpu.VMEM((2, *quarter), BF), pltpu.VMEM(quarter, BF)] * (len(folds) > 0),
        ),
        out_shape=[jax.ShapeDtypeStruct(s, BF) for s in shapes],
        input_output_aliases={1 + len(args) - len(bufs) + j: j for j in range(len(bufs))},
        compiler_params=pltpu.CompilerParams(vmem_limit_bytes=56 * 1024 * 1024),
        cost_estimate=COST if 0 < first < 4 else SMALL,
        name=f"block_{first}",
    )(at, *args)
    return out[:4], *out[4:]


def place_kernel(n_parts, at, *refs):
    parts, out, (held, sems) = refs[:n_parts], refs[-3], refs[-2:]
    n = parts[0].shape[1]
    copies = []
    for j, part in enumerate(parts):
        held[j] = part[...].astype(F32)
        target = out.at[:, pl.ds(pl.multiple_of(at[j] * n, n), n)]
        copies.append(pltpu.make_async_copy(held.at[j], target, sems.at[j]))
        copies[-1].start()
    for copy in copies:
        copy.wait()


def place(at, parts, base=None):
    rows, n = parts[0].shape
    anywhere = pl.BlockSpec(memory_space=pl.ANY)
    some = base is not None
    return pl.pallas_call(
        functools.partial(place_kernel, len(parts)),
        grid_spec=pltpu.PrefetchScalarGridSpec(
            num_scalar_prefetch=1,
            grid=(1,),
            in_specs=[pl.BlockSpec((rows, n), lambda i, at: (0, 0))] * len(parts) + [anywhere] * some,
            out_specs=anywhere,
            scratch_shapes=[pltpu.VMEM((len(parts), rows, n), F32), pltpu.SemaphoreType.DMA((len(parts),))],
        ),
        out_shape=jax.ShapeDtypeStruct((rows, 4 * n), F32),
        input_output_aliases={1 + len(parts): 0} if some else {},
        compiler_params=pltpu.CompilerParams(vmem_limit_bytes=56 * 1024 * 1024),
        cost_estimate=COST,
        name="place",
    )(at, *parts, *([base] * some))


def grad_kernel(n_parts, *refs):
    slopes, ws, terms = refs[:n_parts], refs[n_parts : 2 * n_parts], refs[2 * n_parts : -1]
    total = jnp.dot(slopes[0][...], ws[0][...], preferred_element_type=F32)
    for slope, w in zip(slopes[1:], ws[1:]):
        total += jnp.dot(slope[...], w[...], preferred_element_type=F32)
    for term in terms:
        total += term[...]
    refs[-1][...] = total.astype(refs[-1].dtype)


def token_grad(part, slope, w, terms=(), depth=None, parts=(0,), kind=F32):
    m, n = slope.shape[0] // 2, slope.shape[1]
    d = w.shape[1]
    depth = depth or n
    cols = 512
    tile = pl.BlockSpec((m, cols), lambda i: (0, i))
    return pl.pallas_call(
        functools.partial(grad_kernel, len(parts)),
        grid=(d // cols,),
        in_specs=[
            *[pl.BlockSpec((m, depth), lambda i, k=k: (part, k)) for k in parts],
            *[pl.BlockSpec((depth, cols), lambda i, k=k: (k, i)) for k in parts],
            *([tile] * len(terms)),
        ],
        out_specs=tile,
        out_shape=jax.ShapeDtypeStruct((m, d), kind),
        compiler_params=pltpu.CompilerParams(vmem_limit_bytes=56 * 1024 * 1024),
        cost_estimate=SMALL,
        name=f"token_grad_{part}",
    )(*[slope] * len(parts), *[w] * len(parts), *terms)


def both_grads_kernel(skip, slope, w, before, mine_o, theirs_o):
    m = mine_o.shape[0]
    theirs_o[...] = jnp.dot(slope[m:], w[...], preferred_element_type=F32).astype(BF)
    mine_o[...] = before[...] + jnp.dot(slope[:m, skip:], w[skip:], preferred_element_type=F32)


def both_grads(slope, w, before, skip):
    m, n = slope.shape[0] // 2, slope.shape[1]
    d = w.shape[1]
    cols = 512
    tile = pl.BlockSpec((m, cols), lambda i: (0, i))
    return pl.pallas_call(
        functools.partial(both_grads_kernel, skip),
        grid=(d // cols,),
        in_specs=[
            pl.BlockSpec((2 * m, n), lambda i: (0, 0)),
            pl.BlockSpec((n, cols), lambda i: (0, i)),
            tile,
        ],
        out_specs=[tile, tile],
        out_shape=[jax.ShapeDtypeStruct((m, d), F32), jax.ShapeDtypeStruct((m, d), BF)],
        compiler_params=pltpu.CompilerParams(vmem_limit_bytes=56 * 1024 * 1024),
        cost_estimate=SMALL,
        name="both_grads",
    )(slope, w, before)


def finish_kernel(at, mine, other, *refs):
    i = pl.program_id(0)
    parts, _, out, act, held, sems = refs
    rows = held.shape[2]
    count = held.shape[0]

    def read(k):
        part = parts.at[:, k * rows : (k + 1) * rows]
        return pltpu.make_async_copy(part, held.at[k], sems.at[0, k])

    def write(k):
        target = act.at[:, pl.ds(pl.multiple_of(at[k] * rows, rows), rows)]
        return pltpu.make_async_copy(held.at[k], target, sems.at[1, k])

    @pl.when(i == 0)
    def _():
        for k in range(count):
            read(k).start()

    out[...] = mine[...] + other[...].astype(F32)

    @pl.when(i == 1)
    def _():
        for k in range(count):
            read(k).wait()
            write(k).start()

    @pl.when(i == pl.num_programs(0) - 1)
    def _():
        for k in range(count):
            write(k).wait()


def finish(at, mine, other, act, parts):
    m, d = mine.shape
    rows = ROWS
    tile = pl.BlockSpec((m // 4, d), lambda i, at: (i, 0))
    anywhere = pl.BlockSpec(memory_space=pl.ANY)
    count = parts.shape[1] // rows
    return pl.pallas_call(
        finish_kernel,
        grid_spec=pltpu.PrefetchScalarGridSpec(
            num_scalar_prefetch=1,
            grid=(4,),
            in_specs=[tile, tile] + [anywhere] * 2,
            out_specs=[tile, anywhere],
            scratch_shapes=[pltpu.VMEM((count, m, rows), BF), pltpu.SemaphoreType.DMA((2, count))],
        ),
        out_shape=[jax.ShapeDtypeStruct((m, d), F32), jax.ShapeDtypeStruct(act.shape, BF)],
        input_output_aliases={4: 1},
        compiler_params=pltpu.CompilerParams(vmem_limit_bytes=56 * 1024 * 1024),
        cost_estimate=SMALL,
        name="finish",
    )(at, mine, other, parts, act)


def local(tokens, weight, cotangent):
    m = tokens.shape[0]
    f, r = lax.axis_index("fsdp"), lax.axis_index("rep")
    x, y, zh, zl, c = coords(f, r)
    total_tokens = m * lax.axis_size("fsdp") * lax.axis_size("rep")
    scale = 1.0 / math.sqrt(total_tokens)

    y0, y1 = y % 2, y // 2
    y_half = jnp.where(c == 0, y0 ^ y1, y1)
    y_part = jnp.where(c == 0, y1, y0)

    def columns(c):
        xa = jnp.where(c == 0, x ^ 1, 3 - x)
        xb = jnp.where(c == 0, 3 - x, x ^ 1)
        at_x = {"own": x, "a": xa, "b": xb, "ab": (x + 2) % 4}
        return [
            4 * at_x[name.removesuffix("_z")] + 2 * (1 - zh if name.endswith("_z") else zh) + c for name in ROLES
        ]

    at = jnp.stack([v for col in columns(c) for v in (col, y_half, y_part, y_part ^ c)]).astype(jnp.int32).reshape(len(ROLES), -1)
    at_other = jnp.stack(columns(1 - c)).astype(jnp.int32)
    at_part = jnp.stack([y_part, 1 - y_part]).astype(jnp.int32)

    bufs = ()
    keep, got, got_q = {}, {}, {}

    def meet(*values):
        nonlocal at
        at, *values = lax.optimization_barrier((at, *values))
        return values

    def run(name, *w, fold=(), add=(), kind="halves"):
        nonlocal bufs
        first = ROLES.index(name)
        pairs = [(keep[k], got[k]) for k in fold]
        bufs, *out = block(first, at, tokens, tok_p, w, kind, cotangent, cot_p, add, pairs, bufs, scale)
        return out

    def quarter_to_send(name, row=0):
        return [(keep[name], row, 1), (got[name], row, 1)]

    def total(name, *others, row=0):
        return [(keep[name], row, 0), (got[name], row, 0), got_q[name], *others]

    def only(total, *more):
        def one(terms):
            value = 0.0
            for v, row, col in terms:
                v = v[row * ROWS : (row + 1) * ROWS]
                if col is not None:
                    v = lax.dynamic_slice_in_dim(v, at_part[col] * (v.shape[1] // 2), v.shape[1] // 2, 1)
                value += v.astype(F32)
            return value.astype(BF)

        return jnp.concatenate([one(terms) for terms in (total, *more)]) if more else one(total)

    tok_p = other_core(tokens)
    cot_p = other_core(cotangent)
    own = weight.astype(BF)
    a = x_first(own)
    oz = z_outer(own)

    tok_p, cot_p, own = meet(tok_p, cot_p, own)
    b = x_second(own)
    send, keep["own"] = run("own", own)

    send, a = meet(send, a)
    got["own"], az = y_first(send), z_outer(a)
    send, keep["a"] = run("a", a)

    send, b, got["own"] = meet(send, b, got["own"])
    got["a"], ab = y_first(send), x_first(b)
    send, keep["b"] = run("b", b)

    send, slope, w_all = meet(send, *bufs[2:])
    bufs = [*bufs[:2], slope, w_all]
    grad_o = token_grad(0, slope, w_all, depth=2 * ROWS)
    send, grad_o, ab, got["a"], oz = meet(send, grad_o, ab, got["a"], oz)
    got["b"], bz = y_first(send), x_second(oz)
    send, keep["ab"], q = run("ab", ab, fold=("own", "a"))

    send, q, got["b"], az = meet(send, q, got["b"], az)
    got["ab"], got_two, abz = y_first(send), y_second(q), x_second(az)
    (whole,) = run("a_z", az, kind="whole")

    whole, got["ab"], got_two, bz = meet(whole, got["ab"], got_two, bz)
    got_q["own"], got_q["a"] = (got_two, 0, None), (got_two, 1, None)
    got_two = y_second(only(quarter_to_send("b"), quarter_to_send("ab")))
    whole, abz = meet(whole, abz)
    whole = x_first(whole)
    parts = run("b_z", bz, abz, kind="quarters")

    *parts, got_two = meet(*parts, got_two)
    got_q["b"], got_q["ab"] = (got_two, 0, None), (got_two, 1, None)
    parts = [parts[0], y_second(parts[1]), y_first(parts[2]), y_across(parts[3])]
    got_x = x_second(only(total("b"), total("ab")))
    oz_parts = run("own_z", oz, add=(whole,), kind="quarters")
    act, act_p, slope, w_all = bufs

    *oz_parts, slope, got_x = meet(*oz_parts, slope, got_x)
    got_x1 = x_first(only(total("a", (got_x, 1, None))))
    grad_o, grad_p = both_grads(slope, w_all, grad_o, 2 * ROWS)

    *parts, grad_o, grad_p, got_x, got_x1 = meet(*parts, grad_o, grad_p, got_x, got_x1)
    got_oz = [y_second(oz_parts[1]), y_first(oz_parts[2]), y_across(oz_parts[3])]
    got_x2, got_x3 = (
        permuted(only([(v, row, None) for v in parts])) for row, permuted in enumerate((x_second, x_across))
    )
    same = only(total("own", (got_x, 0, None), (got_x1, 0, None)))

    got_x2, got_x3, *got_oz, grad_o, same = meet(got_x2, got_x3, *got_oz, grad_o, same)
    other = only([(v, 0, None) for v in (oz_parts[0], *got_oz, got_x2, got_x3)])
    other, same, grad_p, act_p = meet(other, same, grad_p, act_p)
    z1, z2, same_z = z_outer(other), z_across(other), z_inner(same)
    swapped, act_p = other_core(grad_p), other_core(act_p)
    input_grad, activated = finish(at_other, grad_o, swapped, act, act_p)

    z1, z2, same_z, input_grad = meet(z1, z2, same_z, input_grad)

    part = sum(v.astype(F32) for v in (same, same_z, z1, z2)).astype(BF)
    here = 2 * y_half + y_part
    across = 2 * (1 - y_half) + (y_part ^ c)
    second_part, first_part = meet(y_second(part), y_first(part))
    last_part = y_first(second_part)
    weight_grad = place(jnp.stack([here, here ^ 1, across]).astype(jnp.int32), [part, second_part, first_part])
    weight_grad, last_part = meet(weight_grad, last_part)
    weight_grad = place((across ^ 1)[None].astype(jnp.int32), [last_part], weight_grad)
    return activated, input_grad, weight_grad


def solution(mesh):
    in_specs = (P(("fsdp", "rep"), None), P("fsdp", None), P(("fsdp", "rep"), None))
    out_specs = (P(("fsdp", "rep"), None), P(("fsdp", "rep"), None), P("fsdp", None))
    return jax.shard_map(local, mesh=mesh, in_specs=in_specs, out_specs=out_specs, check_vma=False)
```
